128 devices in a mesh: row: 8 (over x, y_lo), col: 16 (over y_hi, z, core).
Axes of the slice: x: 4, y: 4 (y_hi: 2, y_lo: 2; y = y_hi * 2 + y_lo), z: 4, core: 2. Of those that a mesh axis runs over, the one named last changes fastest.
Arguments:
- homolog_tensor: float32 [512, 512, 256], P('row', 'col'), may hold values from -6 to 6
- couplings: float32 [512, 512, 128], P('row', 'col'), may hold values from -6 to 6
- attention_probe_matrix: bfloat16 [256, 256], replicated, may hold values from -4 to 4
- attention_extra_matrices: bfloat16 [256, 768], replicated, may hold values from -0.375 to 0.375
- attention_final_matrix: bfloat16 [256, 256], replicated, may hold values from -0.375 to 0.375
- tensor_entry_matrices: bfloat16 [256, 64], replicated, may hold values from -0.375 to 0.375
- tensor_final_matrix: bfloat16 [1024, 128], replicated, may hold values from -4 to 4
- incoming_entry_matrices: bfloat16 [128, 512], replicated, may hold values from -0.5 to 0.5
- incoming_switch_matrix: bfloat16 [128, 128], replicated, may hold values from -0.5 to 0.5
- incoming_final_matrix: bfloat16 [128, 128], replicated, may hold values from -0.5 to 0.5
Outputs:
- refreshed_homologs: float32 [512, 512, 256], P('row', 'col')
- pair_output: float32 [512, 512, 128], P('row', 'col')
The draws below stay inside these ranges and needn't reach their ends.
All inputs are finite; a program needn't handle non-finite values.
Results may differ from the reference program's by a relative error of at most 0.017.
The reference program's roundings to bfloat16 on the way count: a program that leaves them out, or rounds other values in their place, can miss the bound.
Values may be sent and summed in bfloat16 or wider, within the bound.
A program may use at most 128 MiB of HBM per device.

```python
import jax
import jax.numpy as jnp
from jax import lax

FEATURE_DEPTH = 256
C_Z = 128
TENSOR_FEATURES = 32
C_TRI = 128
ATTENTION_UNITS = 8
UNIT_WIDTH = 32
AMINO_LENGTH = 512
HOMOLOG_NUMBER = 512


def draw_attention_probe_matrix(key, part):
    key = jax.random.fold_in(key, 7)
    attended_contents = jnp.clip(jax.random.normal(key, (FEATURE_DEPTH, ATTENTION_UNITS * UNIT_WIDTH), jnp.float32) * FEATURE_DEPTH ** (-0.5), -4.0, 4.0)
    return attended_contents.astype(jnp.bfloat16)


def level_of(own_key, extent, pieces, smallest, top_value):
    def one(position, parts):
        heights = jax.random.uniform(jax.random.fold_in(jax.random.fold_in(own_key, 6), position), (parts,), jnp.float32, smallest / len(pieces), top_value / len(pieces))
        return jnp.repeat(jnp.exp(heights), extent[position] // parts).reshape((-1,) + (1,) * (len(extent) - position - 1))

    loudness = one(*pieces[0])
    for cut in pieces[1:]:
        loudness = loudness * one(*cut)
    return loudness


def bell_draw(stream_key, extent, scale, bound, split=(), dtype=jnp.bfloat16):
    values = jax.random.normal(stream_key, extent, jnp.float32) * scale
    if len(split) > 0:
        values = level_of(stream_key, extent, split, -0.22, 0.18) * values
    return jnp.clip(values, min=-bound, max=bound).astype(dtype)


def setup_inputs(seed: int = 0) -> dict:
    seeds = jax.random.split(jax.random.key(seed), 11)
    homolog_tensor = bell_draw(seeds[0], (HOMOLOG_NUMBER, AMINO_LENGTH, FEATURE_DEPTH), 1.0, 6.0, ((0, 8), (1, 16)), jnp.float32)
    couplings = bell_draw(seeds[1], (AMINO_LENGTH, AMINO_LENGTH, C_Z), 1.0, 6.0, ((0, 8), (1, 16)), jnp.float32)
    attention_probe_matrix = draw_attention_probe_matrix(jax.random.fold_in(seeds[10], 71), 0)
    attention_extra_matrices = bell_draw(seeds[3], (FEATURE_DEPTH, 3 * ATTENTION_UNITS * UNIT_WIDTH), FEATURE_DEPTH ** -0.5, 0.375)
    attention_final_matrix = bell_draw(seeds[4], (ATTENTION_UNITS * UNIT_WIDTH, FEATURE_DEPTH), (ATTENTION_UNITS * UNIT_WIDTH) ** -0.5, 0.375)
    tensor_entry_matrices = bell_draw(seeds[5], (FEATURE_DEPTH, 2 * TENSOR_FEATURES), FEATURE_DEPTH ** -0.5, 0.375)
    tensor_final_matrix = bell_draw(seeds[6], (TENSOR_FEATURES * TENSOR_FEATURES, C_Z), (max(1, TENSOR_FEATURES * TENSOR_FEATURES // HOMOLOG_NUMBER)) ** -0.5, 4.0)
    incoming_entry_matrices = bell_draw(seeds[7], (C_Z, 4 * C_TRI), C_Z ** -0.5, 0.5)
    incoming_switch_matrix = bell_draw(seeds[8], (C_Z, C_Z), C_Z ** -0.5, 0.5)
    incoming_final_matrix = bell_draw(seeds[9], (C_TRI, C_Z), C_TRI ** -0.5, 0.5)
    return dict(homolog_tensor=homolog_tensor, couplings=couplings, attention_probe_matrix=attention_probe_matrix, attention_extra_matrices=attention_extra_matrices, attention_final_matrix=attention_final_matrix, tensor_entry_matrices=tensor_entry_matrices, tensor_final_matrix=tensor_final_matrix, incoming_entry_matrices=incoming_entry_matrices, incoming_switch_matrix=incoming_switch_matrix, incoming_final_matrix=incoming_final_matrix)


def standardise_features(attended_contents):
    centre = lax.optimization_barrier(jnp.mean(attended_contents, axis=-1, keepdims=True))
    centred = attended_contents - centre
    spread = lax.optimization_barrier(jnp.mean(centred * centred, axis=-1, keepdims=True))
    return centred * lax.rsqrt(spread + 1e-05)

def attend_column(column, attention_probe_matrix, attention_extra_matrices):
    homolog_amount = column.shape[0]
    inner_width = ATTENTION_UNITS * UNIT_WIDTH
    queries = (jnp.dot(column, attention_probe_matrix, preferred_element_type=jnp.float32) * UNIT_WIDTH ** (-0.5)).astype(jnp.bfloat16)
    projected_rows = jnp.dot(column, attention_extra_matrices, preferred_element_type=jnp.float32)
    key_rows = projected_rows[:, :inner_width].astype(jnp.bfloat16)
    value_rows = projected_rows[:, inner_width:2 * inner_width].astype(jnp.bfloat16)
    gate_cols = jax.nn.sigmoid(projected_rows[:, 2 * inner_width:])
    queries = queries.reshape(homolog_amount, ATTENTION_UNITS, UNIT_WIDTH).astype(jnp.float32)
    key_rows = key_rows.reshape(homolog_amount, ATTENTION_UNITS, UNIT_WIDTH).astype(jnp.float32)
    value_rows = value_rows.reshape(homolog_amount, ATTENTION_UNITS, UNIT_WIDTH).astype(jnp.float32)
    scores = jnp.einsum('shd,thd->hst', queries, key_rows)
    weights = jax.nn.softmax(scores, axis=-1).astype(jnp.bfloat16)
    attended = jnp.einsum('hst,thd->shd', weights.astype(jnp.float32), value_rows).reshape(homolog_amount, inner_width)
    return (attended * gate_cols).astype(jnp.bfloat16)

def reference(homolog_tensor, couplings, attention_probe_matrix, attention_extra_matrices, attention_final_matrix, tensor_entry_matrices, tensor_final_matrix, incoming_entry_matrices, incoming_switch_matrix, incoming_final_matrix):
    homolog_amount = homolog_tensor.shape[0]
    amino_number = homolog_tensor.shape[1]
    standardised = standardise_features(homolog_tensor).astype(jnp.bfloat16)
    gated = lax.map(lambda column: attend_column(column, attention_probe_matrix, attention_extra_matrices), jnp.transpose(standardised, (1, 0, 2)))
    gated = jnp.transpose(gated, (1, 0, 2))
    residual_change = jnp.dot(gated.reshape(-1, ATTENTION_UNITS * UNIT_WIDTH), attention_final_matrix, preferred_element_type=jnp.float32)
    refreshed_homologs = homolog_tensor + residual_change.reshape(homolog_tensor.shape)
    standardised_result = standardise_features(refreshed_homologs).astype(jnp.bfloat16).reshape(-1, FEATURE_DEPTH)
    projected_rows = jnp.dot(standardised_result, tensor_entry_matrices, preferred_element_type=jnp.float32).astype(jnp.bfloat16)
    projected_rows = projected_rows.reshape(homolog_amount, amino_number, 2 * TENSOR_FEATURES)
    left_alignment = projected_rows[:, :, :TENSOR_FEATURES].reshape(homolog_amount, amino_number * TENSOR_FEATURES)
    right_alignment = projected_rows[:, :, TENSOR_FEATURES:].reshape(homolog_amount, amino_number * TENSOR_FEATURES)
    residue_block = min(64, amino_number)
    left_residue_blocks = jnp.transpose(left_alignment.reshape(homolog_amount, amino_number // residue_block, residue_block * TENSOR_FEATURES), (1, 0, 2))

    def outer_block(left_residue_block):
        outer_product_sum = jnp.dot(left_residue_block.T, right_alignment, preferred_element_type=jnp.float32)
        outer_product_sum = outer_product_sum.reshape(residue_block, TENSOR_FEATURES, amino_number, TENSOR_FEATURES)
        outer_product_sum = jnp.transpose(outer_product_sum, (0, 2, 1, 3)).reshape(residue_block * amino_number, TENSOR_FEATURES * TENSOR_FEATURES)
        outer_mean = (outer_product_sum / homolog_amount).astype(jnp.bfloat16)
        return jnp.dot(outer_mean, tensor_final_matrix, preferred_element_type=jnp.float32).reshape(residue_block, amino_number, C_Z)
    opm_update = lax.map(outer_block, left_residue_blocks).reshape(amino_number, amino_number, C_Z)
    pair_mid = couplings + opm_update
    pair_normed = standardise_features(pair_mid).astype(jnp.bfloat16).reshape(-1, C_Z)
    projected_rows = jnp.dot(pair_normed, incoming_entry_matrices, preferred_element_type=jnp.float32)
    left_pair = (jax.nn.sigmoid(projected_rows[:, C_TRI:2 * C_TRI]) * projected_rows[:, :C_TRI]).astype(jnp.bfloat16)
    right_pair = (jax.nn.sigmoid(projected_rows[:, 3 * C_TRI:]) * projected_rows[:, 2 * C_TRI:3 * C_TRI]).astype(jnp.bfloat16)
    gate_pair = jax.nn.sigmoid(jnp.dot(pair_normed, incoming_switch_matrix, preferred_element_type=jnp.float32))
    left_pair = left_pair.reshape(amino_number, amino_number, C_TRI).astype(jnp.float32)
    right_pair = right_pair.reshape(amino_number, amino_number, C_TRI).astype(jnp.float32)
    product = jnp.einsum('kic,kjc->ijc', left_pair, right_pair)
    product_normed = standardise_features(product).astype(jnp.bfloat16).reshape(-1, C_TRI)
    tri_update = jnp.dot(product_normed, incoming_final_matrix, preferred_element_type=jnp.float32)
    pair_output = pair_mid + (gate_pair * tri_update).reshape(couplings.shape)
    return (refreshed_homologs, pair_output)
```

```python
import functools

import jax
import jax.numpy as jnp
from jax import lax
from jax.experimental import pallas as pl
from jax.experimental.pallas import tpu as pltpu
from jax.sharding import PartitionSpec as P

F32, BF16 = jnp.float32, jnp.bfloat16
MESH = pl.DeviceIdType.MESH
EPS = 1e-05
ROWS, COLS = 8, 16
DEVICES = ROWS * COLS
SEQ, RES = 64, 32
OWN = 4
ALL = 512
FEAT, HEADS = 256, 8
C_Z = 128


def dot(a, b):
    return jnp.dot(a, b, preferred_element_type=F32)


def dot_nt(a, b):
    return lax.dot_general(a, b, (((1,), (1,)), ((), ())), preferred_element_type=F32)


def dot_tn(a, b):
    return lax.dot_general(a, b, (((0,), (0,)), ((), ())), preferred_element_type=F32)


def lane(width):
    return lax.broadcasted_iota(jnp.int32, (1, width), 1)


def head_mask(width, which):
    return jnp.where((lane(width) >> 5) == which, 1.0, 0.0).astype(BF16)


def kernel(
    x_ref, coup_ref, wq_ref, wx_ref, wf_ref, we_ref, wo_ref, wi_ref, wsw_ref, wtri_ref,
    out_m, out_p,
    xs, nt, g, sig, sg, qs, kt, vs, ga, gt, gb, lrs, rb, lb,
    wet, wit, wof, wbd, perm, rf, rp, om, pm, gp, cf, cb, xlr, am, bm, pb, xe, es, er, ef,
    s_x, s_a, r_a, s_sig, r_sig, s_b, r_b, s_l, r_l, s_r, r_r, s_d, r_d, s_e, r_e,
):
    r = lax.axis_index("row")
    c = lax.axis_index("col")
    me = r * COLS + c
    rho = c // 2

    def remote(src, dst, send, recv, row, col):
        return pltpu.make_async_remote_copy(
            src_ref=src, dst_ref=dst, send_sem=send, recv_sem=recv,
            device_id=(row, col), device_id_type=MESH,
        )

    def arrived(ref, sem):
        pltpu.make_async_copy(ref, ref, sem).wait()

    load = [
        pltpu.make_async_copy(x_ref.at[:, pl.ds(k * 128, 128)], xs.at[k], s_x.at[k])
        for k in range(2)
    ]
    load[0].start()
    load[1].start()

    barrier = pltpu.get_barrier_semaphore()

    def greet(d, carry):
        peer = lax.rem(me + d, DEVICES)
        pl.semaphore_signal(
            barrier, inc=1, device_id=(peer // COLS, lax.rem(peer, COLS)), device_id_type=MESH
        )
        return carry

    lax.fori_loop(1, DEVICES, greet, 0)

    def norm_one(q, row, stats):
        n = row * OWN + q
        x0 = xs[0, pl.ds(n, SEQ, stride=RES), :]
        x1 = xs[1, pl.ds(n, SEQ, stride=RES), :]
        mean = jnp.sum(x0 + x1, axis=-1, keepdims=True) * (1.0 / FEAT)
        x0, x1 = x0 - mean, x1 - mean
        var = jnp.sum(x0 * x0 + x1 * x1, axis=-1, keepdims=True) * (1.0 / FEAT) + EPS
        inv = lax.rsqrt(var)
        nt[q, row, :, 0:128] = (x0 * inv).astype(BF16)
        nt[q, row, :, 128:256] = (x1 * inv).astype(BF16)
        sd = var * inv
        high = sd.astype(BF16).astype(F32)
        stats = jnp.where(lane(128) == n, high, stats)
        return jnp.where(lane(128) == n + RES, sd - high, stats)

    load[0].wait()
    load[1].wait()
    stats = jnp.zeros((SEQ, 128), F32)
    for q in range(OWN):
        stats = lax.fori_loop(0, ROWS, lambda row, s, q=q: norm_one(q, row, s), stats)
        if q == 0:
            pl.semaphore_wait(barrier, DEVICES - 1)

        def send_a(j, carry, q=q):
            row = lax.rem(r + j, ROWS)
            remote(nt.at[q, row], g.at[q, r], s_a.at[q], r_a.at[q], row, c).start()
            return carry

        lax.fori_loop(1, ROWS, send_a, 0)
        pltpu.make_async_copy(nt.at[q, r], g.at[q, r], r_a.at[q]).start()
    sig[...] = stats.astype(BF16)

    def send_sig(j, carry):
        row = lax.rem(r + j, ROWS)
        remote(sig, sg.at[r], s_sig, r_sig, row, c).start()
        return carry

    lax.fori_loop(1, ROWS, send_sig, 0)
    pltpu.make_async_copy(sig, sg.at[r], r_sig).start()

    wet[...] = we_ref[...].astype(F32).T.astype(BF16)
    wit[...] = wi_ref[...].astype(F32).T.astype(BF16)
    wof[...] = wo_ref[...].astype(F32)
    wbd[...] = jnp.zeros(wbd.shape, BF16)

    def spread(d, carry):
        block = wof[pl.ds(d, 32, stride=32), :].astype(BF16)
        for a in range(4):
            at = pl.multiple_of(d * 128 + a * 32, 32)
            wbd[pl.ds(at, 32), a * 128 : (a + 1) * 128] = block
        return carry

    lax.fori_loop(0, 32, spread, 0)
    source = lax.broadcasted_iota(jnp.int32, (512, 512), 0)
    target = ((source >> 5) & 3) * 128 + (source >> 7) * 32 + (source & 31)
    column = lax.broadcasted_iota(jnp.int32, (512, 512), 1)
    perm[...] = jnp.where(column == target, 1.0, 0.0).astype(BF16)

    def attend(q, carry):
        arrived(g.at[q], r_a.at[q])
        column = g[q].reshape(ALL, FEAT)
        qs[...] = (dot(column, wq_ref[...]) * 32 ** (-0.5)).astype(BF16)
        kt[...] = dot(column, wx_ref[:, 0:256]).T.astype(BF16)
        vs[...] = dot(column, wx_ref[:, 256:512]).astype(BF16)
        ga[...] = jax.nn.sigmoid(dot(column, wx_ref[:, 512:768]))
        for tile in range(2):
            cols = slice(tile * 128, tile * 128 + 128)
            for part in range(2):
                rows = slice(part * 256, part * 256 + 256)
                top = jnp.zeros((256, 128), F32)
                low = jnp.ones((256, 128), F32)
                for h in range(4):
                    mask = head_mask(128, h)
                    values = vs[:, cols] * mask + (1 - mask)
                    scores = dot(qs[rows, :] * head_mask(256, tile * 4 + h), kt[...])
                    best = jnp.max(scores, axis=-1, keepdims=True)
                    weights = jnp.exp(scores - best).astype(BF16)
                    found = dot(weights, values)
                    here = (lane(128) >> 5) == h
                    top = jnp.where(here, found, top)
                    low = jnp.where(here, pltpu.roll(found, 32, 1), low)
                gated = (top / low * ga[rows, cols]).astype(BF16)
                gt[q, part * 4 : part * 4 + 4, :, cols] = gated.reshape(4, SEQ, 128)

        def send_b(j, carry):
            row = lax.rem(r + j, ROWS)
            remote(gt.at[q, row], gb.at[r * OWN + q], s_b, r_b, row, c).start()
            return carry

        @pl.when(q == 0)
        def _():
            arrived(sg, r_sig)

        for part in range(2):
            rows = slice(part * 256, part * 256 + 256)
            gated = gt[q, part * 4 : part * 4 + 4].reshape(256, FEAT)
            normed = g[q, part * 4 : part * 4 + 4].reshape(256, FEAT).astype(F32)
            spreads = sg[part * 4 : part * 4 + 4].reshape(256, 128).astype(F32)
            n = r * OWN + q
            here = jnp.logical_or(lane(128) == n, lane(128) == n + RES)
            sd = jnp.sum(jnp.where(here, spreads, 0.0), axis=-1, keepdims=True)
            fresh = normed + dot(gated, wf_ref[...]) * (1.0 / sd)
            fresh = fresh - jnp.mean(fresh, axis=-1, keepdims=True)
            var = jnp.mean(fresh * fresh, axis=-1, keepdims=True)
            fresh = (fresh * (sd * lax.rsqrt(sd * sd * var + EPS))).astype(BF16)
            lrs[q, :, rows] = dot_nt(wet[...], fresh).astype(BF16)

        def send_r(j, carry):
            row = lax.rem(r + j, ROWS)
            remote(lrs.at[q, pl.ds(32, 32)], rb.at[r * OWN + q], s_r, r_r, row, c).start()
            return carry

        lax.fori_loop(1, ROWS, send_r, 0)
        pltpu.make_async_copy(lrs.at[q, pl.ds(32, 32)], rb.at[r * OWN + q], r_r).start()
        spot = lax.rem(c, 2) * RES + r * OWN + q

        def send_l(j, carry):
            col = lax.rem(c + j, COLS)
            remote(lrs.at[q, pl.ds(0, 32)], lb.at[spot], s_l, r_l, rho, col).start()
            return carry

        lax.fori_loop(1, COLS, send_l, 0)

        @pl.when(rho == r)
        def _():
            pltpu.make_async_copy(lrs.at[q, pl.ds(0, 32)], lb.at[spot], r_l).start()

        @pl.when(rho != r)
        def _():
            remote(lrs.at[q, pl.ds(0, 32)], lb.at[spot], s_l, r_l, rho, c).start()

        lax.fori_loop(1, ROWS, send_b, 0)
        pltpu.make_async_copy(gt.at[q, r], gb.at[r * OWN + q], r_b).start()
        return carry

    lax.fori_loop(0, OWN, attend, 0)

    arrived(rb, r_r)
    for k in range(4):
        rf[k] = rb[:, :, k * 128 : k * 128 + 128].astype(F32).reshape(1024, 128)

    def by_channel(d, carry):
        at = pl.multiple_of(d * 32, 32)
        for k in range(4):
            rp[pl.ds(at, 32), k * 128 : k * 128 + 128] = rf[
                k, pl.ds(d, 32, stride=32), :
            ].astype(BF16)
        return carry

    lax.fori_loop(0, 32, by_channel, 0)

    arrived(lb, r_l)

    def outer(b, carry):
        left = lb[pl.ds(b * 8, 8)].reshape(256, ALL)
        for d in range(0, 32, 8):
            block = dot_nt(rp[d * 32 : d * 32 + 256, :], left) * (1.0 / ALL)
            block = block.astype(BF16)
            for e in range(8):
                for half in range(2):
                    at = pl.multiple_of(b * 64 + half * 32, 32)
                    om[pl.ds(at, 32), (d + e) * 128 : (d + e + 1) * 128] = block[
                        e * 32 : e * 32 + 32, half * 128 : half * 128 + 128
                    ]
        return carry

    lax.fori_loop(0, 8, outer, 0)

    def mid(b, carry):
        at = pl.multiple_of(b * 128, 128)
        update = dot(om[pl.ds(at, 128), :], wbd[...])
        for e in range(4):
            for a in range(4):
                i = b * 16 + e * 4 + a
                pm[i] = coup_ref[i] + update[e * 32 : e * 32 + 32, a * 128 : a * 128 + 128]
        return carry

    lax.fori_loop(0, 4, mid, 0)

    def entry(b, carry):
        pair = pm[pl.ds(b * 8, 8)].reshape(256, C_Z)
        pair = pair - jnp.mean(pair, axis=-1, keepdims=True)
        var = jnp.mean(pair * pair, axis=-1, keepdims=True)
        pair = (pair * lax.rsqrt(var + EPS)).astype(BF16)
        gp[pl.ds(b * 8, 8)] = jax.nn.sigmoid(dot(pair, wsw_ref[...])).reshape(8, RES, C_Z)
        entries = dot_nt(wit[...], pair)
        left = jax.nn.sigmoid(entries[128:256]) * entries[0:128]
        right = jax.nn.sigmoid(entries[384:512]) * entries[256:384]
        for half in range(2):
            lanes = slice(half * 128, half * 128 + 128)
            t = b * 2 + half
            cf[pl.ds(t, 128, stride=32), :] = left[:, lanes]
            cf[pl.ds(t + 16, 128, stride=32), :] = right[:, lanes]
        return carry

    lax.fori_loop(0, 8, entry, 0)
    cb[...] = cf[...].astype(BF16).reshape(DEVICES, 32, 128)

    corner = r * 4 + c // 4
    lanes_at = pl.multiple_of(lax.rem(c, 4) * 128, 128)

    def send_d(d, carry):
        peer = lax.rem(me + d, DEVICES)
        remote(
            cb.at[peer], xlr.at[corner, :, pl.ds(lanes_at, 128)], s_d, r_d,
            peer // COLS, lax.rem(peer, COLS),
        ).start()
        return carry

    lax.fori_loop(1, DEVICES, send_d, 0)
    pltpu.make_async_copy(cb.at[me], xlr.at[corner, :, pl.ds(lanes_at, 128)], r_d).start()

    arrived(gb, r_b)

    def refresh(n, carry):
        where = pl.ds(n, SEQ, stride=RES)
        change = dot(gb[n], wf_ref[...])
        for k in range(2):
            xs[k, where, :] = xs[k, where, :] + change[:, k * 128 : k * 128 + 128]
        return carry

    lax.fori_loop(0, RES, refresh, 0)
    store = [
        pltpu.make_async_copy(xs.at[k], out_m.at[:, pl.ds(k * 128, 128)], s_x.at[k])
        for k in range(2)
    ]
    store[0].start()
    store[1].start()

    arrived(xlr, r_d)

    def line_up(b, carry):
        moved = dot(xlr[pl.ds(b * 4, 4)].reshape(128, 512), perm[...]).astype(BF16)
        for e in range(4):
            for a in range(4):
                at = pl.multiple_of(b * 64 + a * 16, 16)
                lanes = slice(a * 128, a * 128 + 128)
                spot = slice(e * 128, e * 128 + 128)
                am[pl.ds(at, 16), spot] = moved[e * 32 : e * 32 + 16, lanes]
                bm[pl.ds(at, 16), spot] = moved[e * 32 + 16 : e * 32 + 32, lanes]
        return carry

    lax.fori_loop(0, 8, line_up, 0)
    pb[...] = dot_tn(am[...], bm[...]).astype(BF16)

    def deal(b, carry):
        for e in range(4):
            for a in range(4):
                at = pl.multiple_of(b * 64 + a * 16, 16)
                xe[e * 16 : e * 16 + 16, a * 128 : a * 128 + 128] = pb[
                    pl.ds(at, 16), e * 128 : e * 128 + 128
                ]
        es[pl.ds(b * 4, 4)] = dot(xe[...], perm[...]).astype(BF16).reshape(4, 16, 512)
        return carry

    lax.fori_loop(0, 8, deal, 0)

    def piece(peer):
        row, col = peer // COLS, lax.rem(peer, COLS)
        at = pl.multiple_of(lax.rem(col, 4) * 128, 128)
        return es.at[row * 4 + col // 4, :, pl.ds(at, 128)]

    def send_e(d, carry):
        peer = lax.rem(me + d, DEVICES)
        remote(
            piece(peer), er.at[me], s_e, r_e, peer // COLS, lax.rem(peer, COLS)
        ).start()
        return carry

    lax.fori_loop(1, DEVICES, send_e, 0)
    pltpu.make_async_copy(piece(me), er.at[me], r_e).start()
    arrived(er, r_e)

    ef[...] = er[...].astype(F32).reshape(DEVICES * 16, 128)

    def final(t, carry):
        prod = ef[pl.ds(t, DEVICES, stride=16), :]
        prod = prod - jnp.mean(prod, axis=0, keepdims=True)
        var = jnp.mean(prod * prod, axis=0, keepdims=True)
        prod = (prod * lax.rsqrt(var + EPS)).astype(BF16)
        update = dot_tn(prod, wtri_ref[...])
        for a in range(4):
            i = a * 16 + t
            out_p[i] = pm[i] + gp[i] * update[a * 32 : a * 32 + 32]
        return carry

    lax.fori_loop(0, 16, final, 0)

    store[0].wait()
    store[1].wait()
    for q in range(OWN):
        arrived(nt.at[q, pl.ds(0, 7)], s_a.at[q])
    arrived(sg.at[pl.ds(0, 7)], s_sig)
    arrived(gb.at[pl.ds(0, 28)], s_b)
    arrived(rb.at[pl.ds(0, 28)], s_r)

    @pl.when(rho == r)
    def _():
        arrived(lb.at[pl.ds(0, 60)], s_l)

    @pl.when(rho != r)
    def _():
        arrived(lb, s_l)

    arrived(cb.at[pl.ds(0, DEVICES - 1)], s_d)
    arrived(er.at[pl.ds(0, DEVICES - 1)], s_e)


def body(x, coup, wq, wx, wf, we, wo, wi, wsw, wtri):
    vmem = pl.BlockSpec(memory_space=pltpu.VMEM)
    hbm = pl.BlockSpec(memory_space=pl.ANY)
    dma = pltpu.SemaphoreType.DMA
    out_m, out_p = pl.pallas_call(
        kernel,
        out_shape=(
            jax.ShapeDtypeStruct((SEQ * RES, FEAT), F32),
            jax.ShapeDtypeStruct((SEQ, RES, C_Z), F32),
        ),
        in_specs=[hbm] + [vmem] * 9,
        out_specs=(hbm, vmem),
        scratch_shapes=[
            pltpu.VMEM((2, SEQ * RES, 128), F32),
            pltpu.VMEM((OWN, ROWS, SEQ, FEAT), BF16),
            pltpu.VMEM((OWN, ROWS, SEQ, FEAT), BF16),
            pltpu.VMEM((SEQ, 128), BF16),
            pltpu.VMEM((ROWS, SEQ, 128), BF16),
            pltpu.VMEM((ALL, FEAT), BF16),
            pltpu.VMEM((FEAT, ALL), BF16),
            pltpu.VMEM((ALL, FEAT), BF16),
            pltpu.VMEM((ALL, FEAT), F32),
            pltpu.VMEM((OWN, ROWS, SEQ, FEAT), BF16),
            pltpu.VMEM((RES, SEQ, FEAT), BF16),
            pltpu.VMEM((OWN, 64, ALL), BF16),
            pltpu.VMEM((RES, 32, ALL), BF16),
            pltpu.VMEM((SEQ, 32, ALL), BF16),
            pltpu.VMEM((64, FEAT), BF16),
            pltpu.VMEM((512, C_Z), BF16),
            pltpu.VMEM((1024, C_Z), F32),
            pltpu.VMEM((4096, 512), BF16),
            pltpu.VMEM((512, 512), BF16),
            pltpu.VMEM((4, 1024, 128), F32),
            pltpu.VMEM((1024, ALL), BF16),
            pltpu.VMEM((512, 4096), BF16),
            pltpu.VMEM((SEQ, RES, C_Z), F32),
            pltpu.VMEM((SEQ, RES, C_Z), F32),
            pltpu.VMEM((DEVICES * 32, 128), F32),
            pltpu.VMEM((DEVICES, 32, 128), BF16),
            pltpu.VMEM((32, 32, 512), BF16),
            pltpu.VMEM((512, 512), BF16),
            pltpu.VMEM((512, 512), BF16),
            pltpu.VMEM((512, 512), BF16),
            pltpu.VMEM((64, 512), BF16),
            pltpu.VMEM((32, 16, 512), BF16),
            pltpu.VMEM((DEVICES, 16, 128), BF16),
            pltpu.VMEM((DEVICES * 16, 128), F32),
            dma((2,)),
            dma((OWN,)), dma((OWN,)),
            dma(()), dma(()),
            dma(()), dma(()),
            dma(()), dma(()),
            dma(()), dma(()),
            dma(()), dma(()),
            dma(()), dma(()),
        ],
        compiler_params=pltpu.CompilerParams(
            collective_id=0, has_side_effects=True, vmem_limit_bytes=56 * 2**20
        ),
    )(x.reshape(SEQ * RES, FEAT), coup, wq, wx, wf, we, wo, wi, wsw, wtri)
    return out_m.reshape(SEQ, RES, FEAT), out_p


def solution(mesh):
    spread = P("row", "col", None)
    return jax.shard_map(
        body, mesh=mesh, in_specs=(spread, spread) + (P(),) * 8,
        out_specs=(spread, spread), check_vma=False,
    )
```

```python
import functools

import jax
import jax.numpy as jnp
from jax import lax
from jax.experimental import pallas as pl
from jax.experimental.pallas import tpu as pltpu
from jax.sharding import PartitionSpec as P

F32, BF16 = jnp.float32, jnp.bfloat16
MESH = pl.DeviceIdType.MESH
EPS = 1e-05
ROWS, COLS = 8, 16
DEVICES = ROWS * COLS
SEQ, RES = 64, 32
OWN = 4
ALL = 512
FEAT, HEADS = 256, 8
C_Z = 128


def dot(a, b):
    return jnp.dot(a, b, preferred_element_type=F32)


def dot_nt(a, b):
    return lax.dot_general(a, b, (((1,), (1,)), ((), ())), preferred_element_type=F32)


def dot_tn(a, b):
    return lax.dot_general(a, b, (((0,), (0,)), ((), ())), preferred_element_type=F32)


def lane(width):
    return lax.broadcasted_iota(jnp.int32, (1, width), 1)


def head_mask(width, which):
    return jnp.where((lane(width) >> 5) == which, 1.0, 0.0).astype(BF16)


def kernel(
    x_ref, coup_ref, wq_ref, wx_ref, wf_ref, we_ref, wo_ref, wi_ref, wsw_ref, wtri_ref,
    out_m, out_p,
    xs, nt, g, sig, sg, qs, kt, vs, ga, gt, gb, lrs, rb, lb,
    wit, wof, wbd, perm, rf, rp, om, pm, gp, cf, cb, xlr, am, bm, pb, xe, es, er, ef,
    s_x, s_a, r_a, s_sig, r_sig, s_b, r_b, s_h, r_h, s_l, r_l, s_r, r_r, s_d, r_d, s_e, r_e,
):
    r = lax.axis_index("row")
    c = lax.axis_index("col")
    me = r * COLS + c
    rho = c // 2

    def remote(src, dst, send, recv, row, col):
        return pltpu.make_async_remote_copy(
            src_ref=src, dst_ref=dst, send_sem=send, recv_sem=recv,
            device_id=(row, col), device_id_type=MESH,
        )

    def arrived(ref, sem):
        pltpu.make_async_copy(ref, ref, sem).wait()

    load = [
        pltpu.make_async_copy(x_ref.at[:, pl.ds(k * 128, 128)], xs.at[k], s_x.at[k])
        for k in range(2)
    ]
    load[0].start()
    load[1].start()

    barrier = pltpu.get_barrier_semaphore()

    def greet(d, carry):
        peer = lax.rem(me + d, DEVICES)
        pl.semaphore_signal(
            barrier, inc=1, device_id=(peer // COLS, lax.rem(peer, COLS)), device_id_type=MESH
        )
        return carry

    lax.fori_loop(1, DEVICES, greet, 0)

    def norm_one(q, row, stats):
        n = row * OWN + q
        x0 = xs[0, pl.ds(n, SEQ, stride=RES), :]
        x1 = xs[1, pl.ds(n, SEQ, stride=RES), :]
        mean = jnp.sum(x0 + x1, axis=-1, keepdims=True) * (1.0 / FEAT)
        x0, x1 = x0 - mean, x1 - mean
        var = jnp.sum(x0 * x0 + x1 * x1, axis=-1, keepdims=True) * (1.0 / FEAT) + EPS
        inv = lax.rsqrt(var)
        nt[q, row, :, 0:128] = (x0 * inv).astype(BF16)
        nt[q, row, :, 128:256] = (x1 * inv).astype(BF16)
        sd = var * inv
        high = sd.astype(BF16).astype(F32)
        stats = jnp.where(lane(128) == n, high, stats)
        return jnp.where(lane(128) == n + RES, sd - high, stats)

    load[0].wait()
    load[1].wait()
    stats = jnp.zeros((SEQ, 128), F32)
    for q in range(OWN):
        stats = lax.fori_loop(0, ROWS, lambda row, s, q=q: norm_one(q, row, s), stats)
        if q == 0:
            pl.semaphore_wait(barrier, DEVICES - 1)

        def send_a(j, carry, q=q):
            row = lax.rem(r + j, ROWS)
            remote(nt.at[q, row], g.at[q, r], s_a.at[q], r_a.at[q], row, c).start()
            return carry

        lax.fori_loop(1, ROWS, send_a, 0)
        pltpu.make_async_copy(nt.at[q, r], g.at[q, r], r_a.at[q]).start()
    sig[...] = stats.astype(BF16)

    def send_sig(j, carry):
        row = lax.rem(r + j, ROWS)
        remote(sig, sg.at[r], s_sig, r_sig, row, c).start()
        return carry

    lax.fori_loop(1, ROWS, send_sig, 0)
    pltpu.make_async_copy(sig, sg.at[r], r_sig).start()

    wit[...] = wi_ref[...].astype(F32).T.astype(BF16)
    wof[...] = wo_ref[...].astype(F32)
    wbd[...] = jnp.zeros(wbd.shape, BF16)

    def spread(d, carry):
        block = wof[pl.ds(d, 32, stride=32), :].astype(BF16)
        for a in range(4):
            at = pl.multiple_of(d * 128 + a * 32, 32)
            wbd[pl.ds(at, 32), a * 128 : (a + 1) * 128] = block
        return carry

    lax.fori_loop(0, 32, spread, 0)
    source = lax.broadcasted_iota(jnp.int32, (512, 512), 0)
    target = ((source >> 5) & 3) * 128 + (source >> 7) * 32 + (source & 31)
    column = lax.broadcasted_iota(jnp.int32, (512, 512), 1)
    perm[...] = jnp.where(column == target, 1.0, 0.0).astype(BF16)

    def relay(q):
        arrived(lb.at[pl.ds(0, 2)], r_h.at[q])

        def pass_on(j, carry):
            col = c // 8 * 8 + lax.rem(c + j, 8)
            for side in range(2):
                spot = q * 16 + side * 8 + lax.rem(c, 8)
                remote(lb.at[spot], lb.at[spot], s_l, r_l.at[q], r, col).start()
            return carry

        lax.fori_loop(1, 8, pass_on, 0)

    def attend(q, carry):
        arrived(g.at[q], r_a.at[q])
        column = g[q].reshape(ALL, FEAT)
        qs[...] = (dot(column, wq_ref[...]) * 32 ** (-0.5)).astype(BF16)
        kt[...] = dot(column, wx_ref[:, 0:256]).T.astype(BF16)
        vs[...] = dot(column, wx_ref[:, 256:512]).astype(BF16)
        ga[...] = jax.nn.sigmoid(dot(column, wx_ref[:, 512:768]))
        for tile in range(2):
            if tile == 1:

                @pl.when(q > 0)
                def _():
                    relay(q - 1)

            cols = slice(tile * 128, tile * 128 + 128)
            for part in range(2):
                rows = slice(part * 256, part * 256 + 256)
                top = jnp.zeros((256, 128), F32)
                low = jnp.ones((256, 128), F32)
                for h in range(4):
                    mask = head_mask(128, h)
                    values = vs[:, cols] * mask + (1 - mask)
                    scores = dot(qs[rows, :] * head_mask(256, tile * 4 + h), kt[...])
                    best = jnp.max(scores, axis=-1, keepdims=True)
                    weights = jnp.exp(scores - best).astype(BF16)
                    found = dot(weights, values)
                    here = (lane(128) >> 5) == h
                    top = jnp.where(here, found, top)
                    low = jnp.where(here, pltpu.roll(found, 32, 1), low)
                gated = (top / low * ga[rows, cols]).astype(BF16)
                gt[q, part * 4 : part * 4 + 4, :, cols] = gated.reshape(4, SEQ, 128)

        def send_b(j, carry):
            row = lax.rem(r + j, ROWS)
            remote(gt.at[q, row], gb.at[r * OWN + q], s_b, r_b, row, c).start()
            return carry

        @pl.when(q == 0)
        def _():
            arrived(sg, r_sig)

        for part in range(2):
            rows = slice(part * 256, part * 256 + 256)
            gated = gt[q, part * 4 : part * 4 + 4].reshape(256, FEAT)
            normed = g[q, part * 4 : part * 4 + 4].reshape(256, FEAT).astype(F32)
            spreads = sg[part * 4 : part * 4 + 4].reshape(256, 128).astype(F32)
            n = r * OWN + q
            here = jnp.logical_or(lane(128) == n, lane(128) == n + RES)
            sd = jnp.sum(jnp.where(here, spreads, 0.0), axis=-1, keepdims=True)
            fresh = normed + dot(gated, wf_ref[...]) * (1.0 / sd)
            fresh = fresh - jnp.mean(fresh, axis=-1, keepdims=True)
            var = jnp.mean(fresh * fresh, axis=-1, keepdims=True)
            fresh = (fresh * (sd * lax.rsqrt(sd * sd * var + EPS))).astype(BF16)
            lrs[q, :, rows] = dot_nt(we_ref[...], fresh).astype(BF16)

        def send_r(j, carry):
            row = lax.rem(r + j, ROWS)
            remote(lrs.at[q, pl.ds(32, 32)], rb.at[r * OWN + q], s_r, r_r, row, c).start()
            return carry

        lax.fori_loop(1, ROWS, send_r, 0)
        pltpu.make_async_copy(lrs.at[q, pl.ds(32, 32)], rb.at[r * OWN + q], r_r).start()
        spot = q * 16 + lax.rem(c, 2) * ROWS + r
        for half in range(2):
            here = jnp.logical_and(rho == r, c == half * 8 + r)

            @pl.when(here)
            def _():
                pltpu.make_async_copy(lrs.at[q, pl.ds(0, 32)], lb.at[spot], r_h.at[q]).start()

            @pl.when(jnp.logical_not(here))
            def _():
                remote(
                    lrs.at[q, pl.ds(0, 32)], lb.at[spot], s_h, r_h.at[q], rho, half * 8 + r
                ).start()

        lax.fori_loop(1, ROWS, send_b, 0)
        pltpu.make_async_copy(gt.at[q, r], gb.at[r * OWN + q], r_b).start()
        return carry

    lax.fori_loop(0, OWN, attend, 0)

    arrived(rb, r_r)
    for k in range(4):
        rf[k] = rb[:, :, k * 128 : k * 128 + 128].astype(F32).reshape(1024, 128)

    def by_channel(d, carry):
        at = pl.multiple_of(d * 32, 32)
        for k in range(4):
            rp[pl.ds(at, 32), k * 128 : k * 128 + 128] = rf[
                k, pl.ds(d, 32, stride=32), :
            ].astype(BF16)
        return carry

    lax.fori_loop(0, 32, by_channel, 0)

    relay(OWN - 1)

    def outer(b, carry):
        left = lb[pl.ds(b * 8, 8)].reshape(256, ALL)
        for d in range(0, 32, 8):
            block = dot_nt(rp[d * 32 : d * 32 + 256, :], left) * (1.0 / ALL)
            block = block.astype(BF16)
            for e in range(8):
                for half in range(2):
                    at = pl.multiple_of(b * 64 + half * 32, 32)
                    om[pl.ds(at, 32), (d + e) * 128 : (d + e + 1) * 128] = block[
                        e * 32 : e * 32 + 32, half * 128 : half * 128 + 128
                    ]
        return carry

    def mid(b, carry):
        at = pl.multiple_of(b * 128, 128)
        update = dot(om[pl.ds(at, 128), :], wbd[...])
        for e in range(4):
            for a in range(4):
                i = e // 2 * 32 + (e % 2 * 4 + a) * 4 + b
                pm[b * 16 + e * 4 + a] = coup_ref[i] + update[e * 32 : e * 32 + 32, a * 128 : a * 128 + 128]
        return carry

    def entry(b, carry):
        pair = pm[pl.ds(b * 8, 8)].reshape(256, C_Z)
        pair = pair - jnp.mean(pair, axis=-1, keepdims=True)
        var = jnp.mean(pair * pair, axis=-1, keepdims=True)
        pair = (pair * lax.rsqrt(var + EPS)).astype(BF16)
        gp[pl.ds(b * 8, 8)] = jax.nn.sigmoid(dot(pair, wsw_ref[...])).reshape(8, RES, C_Z)
        entries = dot_nt(wit[...], pair)
        left = jax.nn.sigmoid(entries[128:256]) * entries[0:128]
        right = jax.nn.sigmoid(entries[384:512]) * entries[256:384]
        for half in range(2):
            lanes = slice(half * 128, half * 128 + 128)
            t = b * 2 + half
            cf[pl.ds(t, 128, stride=32), :] = left[:, lanes]
            cf[pl.ds(t + 16, 128, stride=32), :] = right[:, lanes]
        return carry

    def pairs(q, carry):
        arrived(lb.at[pl.ds(0, 14)], r_l.at[q])
        lax.fori_loop(q * 2, q * 2 + 2, outer, 0)
        mid(q, 0)
        lax.fori_loop(q * 2, q * 2 + 2, entry, 0)
        return carry

    lax.fori_loop(0, OWN, pairs, 0)
    cb[...] = cf[...].astype(BF16).reshape(DEVICES, 32, 128)

    corner = r * 4 + c // 4
    lanes_at = pl.multiple_of(lax.rem(c, 4) * 128, 128)

    def send_d(d, carry):
        peer = lax.rem(me + d, DEVICES)
        remote(
            cb.at[peer], xlr.at[corner, :, pl.ds(lanes_at, 128)], s_d, r_d,
            peer // COLS, lax.rem(peer, COLS),
        ).start()
        return carry

    lax.fori_loop(1, DEVICES, send_d, 0)
    pltpu.make_async_copy(cb.at[me], xlr.at[corner, :, pl.ds(lanes_at, 128)], r_d).start()

    arrived(gb, r_b)

    def refresh(n, carry):
        where = pl.ds(n, SEQ, stride=RES)
        change = dot(gb[n], wf_ref[...])
        for k in range(2):
            xs[k, where, :] = xs[k, where, :] + change[:, k * 128 : k * 128 + 128]
        return carry

    lax.fori_loop(0, RES, refresh, 0)
    store = [
        pltpu.make_async_copy(xs.at[k], out_m.at[:, pl.ds(k * 128, 128)], s_x.at[k])
        for k in range(2)
    ]
    store[0].start()
    store[1].start()

    arrived(xlr, r_d)

    def line_up(b, carry):
        moved = dot(xlr[pl.ds(b * 4, 4)].reshape(128, 512), perm[...]).astype(BF16)
        for e in range(4):
            for a in range(4):
                at = pl.multiple_of(b * 64 + a * 16, 16)
                lanes = slice(a * 128, a * 128 + 128)
                spot = slice(e * 128, e * 128 + 128)
                am[pl.ds(at, 16), spot] = moved[e * 32 : e * 32 + 16, lanes]
                bm[pl.ds(at, 16), spot] = moved[e * 32 + 16 : e * 32 + 32, lanes]
        return carry

    lax.fori_loop(0, 8, line_up, 0)
    pb[...] = dot_tn(am[...], bm[...]).astype(BF16)

    def deal(b, carry):
        for e in range(4):
            for a in range(4):
                at = pl.multiple_of(b * 64 + a * 16, 16)
                xe[e * 16 : e * 16 + 16, a * 128 : a * 128 + 128] = pb[
                    pl.ds(at, 16), e * 128 : e * 128 + 128
                ]
        es[pl.ds(b * 4, 4)] = dot(xe[...], perm[...]).astype(BF16).reshape(4, 16, 512)
        return carry

    lax.fori_loop(0, 8, deal, 0)

    def piece(peer):
        row, col = peer // COLS, lax.rem(peer, COLS)
        at = pl.multiple_of(lax.rem(col, 4) * 128, 128)
        return es.at[row * 4 + col // 4, :, pl.ds(at, 128)]

    def send_e(d, carry):
        peer = lax.rem(me + d, DEVICES)
        remote(
            piece(peer), er.at[me], s_e, r_e, peer // COLS, lax.rem(peer, COLS)
        ).start()
        return carry

    lax.fori_loop(1, DEVICES, send_e, 0)
    pltpu.make_async_copy(piece(me), er.at[me], r_e).start()
    arrived(er, r_e)

    ef[...] = er[...].astype(F32).reshape(DEVICES * 16, 128)

    def final(t, carry):
        prod = ef[pl.ds(t, DEVICES, stride=16), :]
        prod = prod - jnp.mean(prod, axis=0, keepdims=True)
        var = jnp.mean(prod * prod, axis=0, keepdims=True)
        prod = (prod * lax.rsqrt(var + EPS)).astype(BF16)
        update = dot_tn(prod, wtri_ref[...])
        for a in range(4):
            p = lax.rem(t, 4) * 16 + a * 4 + t // 4
            out_p[a * 16 + t] = pm[p] + gp[p] * update[a * 32 : a * 32 + 32]
        return carry

    lax.fori_loop(0, 16, final, 0)

    store[0].wait()
    store[1].wait()
    for q in range(OWN):
        arrived(nt.at[q, pl.ds(0, 7)], s_a.at[q])
    arrived(sg.at[pl.ds(0, 7)], s_sig)
    arrived(gb.at[pl.ds(0, 28)], s_b)
    arrived(rb.at[pl.ds(0, 28)], s_r)

    relays_itself = jnp.logical_and(rho == r, lax.rem(c, 8) == r)

    @pl.when(relays_itself)
    def _():
        arrived(lb.at[pl.ds(0, 4)], s_h)

    @pl.when(jnp.logical_not(relays_itself))
    def _():
        arrived(lb.at[pl.ds(0, 8)], s_h)

    arrived(lb.at[pl.ds(0, 56)], s_l)
    arrived(cb.at[pl.ds(0, DEVICES - 1)], s_d)
    arrived(er.at[pl.ds(0, DEVICES - 1)], s_e)


def body(x, coup, wq, wx, wf, we, wo, wi, wsw, wtri):
    vmem = pl.BlockSpec(memory_space=pltpu.VMEM)
    hbm = pl.BlockSpec(memory_space=pl.ANY)
    dma = pltpu.SemaphoreType.DMA
    out_m, out_p = pl.pallas_call(
        kernel,
        out_shape=(
            jax.ShapeDtypeStruct((SEQ * RES, FEAT), F32),
            jax.ShapeDtypeStruct((SEQ, RES, C_Z), F32),
        ),
        in_specs=[hbm] + [vmem] * 9,
        out_specs=(hbm, vmem),
        scratch_shapes=[
            pltpu.VMEM((2, SEQ * RES, 128), F32),
            pltpu.VMEM((OWN, ROWS, SEQ, FEAT), BF16),
            pltpu.VMEM((OWN, ROWS, SEQ, FEAT), BF16),
            pltpu.VMEM((SEQ, 128), BF16),
            pltpu.VMEM((ROWS, SEQ, 128), BF16),
            pltpu.VMEM((ALL, FEAT), BF16),
            pltpu.VMEM((FEAT, ALL), BF16),
            pltpu.VMEM((ALL, FEAT), BF16),
            pltpu.VMEM((ALL, FEAT), F32),
            pltpu.VMEM((OWN, ROWS, SEQ, FEAT), BF16),
            pltpu.VMEM((RES, SEQ, FEAT), BF16),
            pltpu.VMEM((OWN, 64, ALL), BF16),
            pltpu.VMEM((RES, 32, ALL), BF16),
            pltpu.VMEM((SEQ, 32, ALL), BF16),
            pltpu.VMEM((512, C_Z), BF16),
            pltpu.VMEM((1024, C_Z), F32),
            pltpu.VMEM((4096, 512), BF16),
            pltpu.VMEM((512, 512), BF16),
            pltpu.VMEM((4, 1024, 128), F32),
            pltpu.VMEM((1024, ALL), BF16),
            pltpu.VMEM((512, 4096), BF16),
            pltpu.VMEM((SEQ, RES, C_Z), F32),
            pltpu.VMEM((SEQ, RES, C_Z), F32),
            pltpu.VMEM((DEVICES * 32, 128), F32),
            pltpu.VMEM((DEVICES, 32, 128), BF16),
            pltpu.VMEM((32, 32, 512), BF16),
            pltpu.VMEM((512, 512), BF16),
            pltpu.VMEM((512, 512), BF16),
            pltpu.VMEM((512, 512), BF16),
            pltpu.VMEM((64, 512), BF16),
            pltpu.VMEM((32, 16, 512), BF16),
            pltpu.VMEM((DEVICES, 16, 128), BF16),
            pltpu.VMEM((DEVICES * 16, 128), F32),
            dma((2,)),
            dma((OWN,)), dma((OWN,)),
            dma(()), dma(()),
            dma(()), dma(()),
            dma(()), dma((OWN,)),
            dma(()), dma((OWN,)),
            dma(()), dma(()),
            dma(()), dma(()),
            dma(()), dma(()),
        ],
        compiler_params=pltpu.CompilerParams(
            collective_id=0, has_side_effects=True, vmem_limit_bytes=56 * 2**20
        ),
    )(x.reshape(SEQ * RES, FEAT), coup, wq, wx, wf, we.T, wo, wi, wsw, wtri)
    return out_m.reshape(SEQ, RES, FEAT), out_p


def solution(mesh):
    spread = P("row", "col", None)
    return jax.shard_map(
        body, mesh=mesh, in_specs=(spread, spread) + (P(),) * 8,
        out_specs=(spread, spread), check_vma=False,
    )
```

```python
import functools

import jax
import jax.numpy as jnp
from jax import lax
from jax.experimental import pallas as pl
from jax.experimental.pallas import tpu as pltpu
from jax.sharding import PartitionSpec as P

F32, BF16 = jnp.float32, jnp.bfloat16
MESH = pl.DeviceIdType.MESH
EPS = 1e-05
LOG2E = 1.4426950408889634
ROWS, COLS = 8, 16
DEVICES = ROWS * COLS
SEQ, RES = 64, 32
OWN = 4
ALL = 512
FEAT, HEADS = 256, 8
C_Z = 128


def dot(a, b):
    return jnp.dot(a, b, preferred_element_type=F32)


def dot_nt(a, b):
    return lax.dot_general(a, b, (((1,), (1,)), ((), ())), preferred_element_type=F32)


def dot_tn(a, b):
    return lax.dot_general(a, b, (((0,), (0,)), ((), ())), preferred_element_type=F32)


def lane(width):
    return lax.broadcasted_iota(jnp.int32, (1, width), 1)


def head_mask(width, which):
    return jnp.where((lane(width) >> 5) == which, 1.0, 0.0).astype(BF16)


def kernel(
    x_ref, coup_ref, wq_ref, wx_ref, wf_ref, we_ref, wo_ref, wi_ref, wsw_ref, wtri_ref,
    out_m, out_p,
    xs, nt, g, sig, sg, qs, kt, vs, ga, gt, gb, lrs, rb, lb,
    wit, wof, wbd, perm, rf, rp, om, pm, gp, cf, cb, xlr, am, bm, pa, pb, xe, es, er, ef,
    s_x, s_a, r_a, s_sig, r_sig, s_b, r_b, s_h, r_h, s_l, r_l, s_c, r_c, s_r, r_r, s_d, r_d, s_e, r_e,
):
    r = lax.axis_index("row")
    c = lax.axis_index("col")
    me = r * COLS + c
    rho = c // 2

    def remote(src, dst, send, recv, row, col):
        return pltpu.make_async_remote_copy(
            src_ref=src, dst_ref=dst, send_sem=send, recv_sem=recv,
            device_id=(row, col), device_id_type=MESH,
        )

    def arrived(ref, sem):
        pltpu.make_async_copy(ref, ref, sem).wait()

    load = [
        pltpu.make_async_copy(x_ref.at[:, pl.ds(k * 128, 128)], xs.at[k], s_x.at[k])
        for k in range(2)
    ]
    load[0].start()
    load[1].start()

    barrier = pltpu.get_barrier_semaphore()

    def greet(d, carry):
        peer = lax.rem(me + d, DEVICES)
        pl.semaphore_signal(
            barrier, inc=1, device_id=(peer // COLS, lax.rem(peer, COLS)), device_id_type=MESH
        )
        return carry

    lax.fori_loop(1, DEVICES, greet, 0)

    def norm_one(q, row, stats):
        n = row * OWN + q
        x0 = xs[0, pl.ds(n, SEQ, stride=RES), :]
        x1 = xs[1, pl.ds(n, SEQ, stride=RES), :]
        mean = jnp.sum(x0 + x1, axis=-1, keepdims=True) * (1.0 / FEAT)
        x0, x1 = x0 - mean, x1 - mean
        var = jnp.sum(x0 * x0 + x1 * x1, axis=-1, keepdims=True) * (1.0 / FEAT) + EPS
        inv = lax.rsqrt(var)
        nt[q, row, :, 0:128] = (x0 * inv).astype(BF16)
        nt[q, row, :, 128:256] = (x1 * inv).astype(BF16)
        sd = var * inv
        high = sd.astype(BF16).astype(F32)
        stats = jnp.where(lane(128) == n, high, stats)
        return jnp.where(lane(128) == n + RES, sd - high, stats)

    load[0].wait()
    load[1].wait()
    def send_normed(q):
        def send_a(j, carry):
            row = lax.rem(r + j, ROWS)
            remote(nt.at[q, row], g.at[q, r], s_a.at[q], r_a.at[q], row, c).start()
            return carry

        lax.fori_loop(1, ROWS, send_a, 0)
        pltpu.make_async_copy(nt.at[q, r], g.at[q, r], r_a.at[q]).start()

    def send_sig(j, carry):
        row = lax.rem(r + j, ROWS)
        remote(sig, sg.at[r], s_sig, r_sig, row, c).start()
        return carry

    stats = jnp.zeros((SEQ, 128), F32)
    for q in range(OWN):
        stats = lax.fori_loop(0, ROWS, lambda row, s, q=q: norm_one(q, row, s), stats, unroll=4)
        if q == 0:
            pl.semaphore_wait(barrier, DEVICES - 1)
            send_normed(0)
    sig[...] = stats.astype(BF16)

    wit[...] = wi_ref[...].astype(F32).T.astype(BF16)
    wof[...] = wo_ref[...].astype(F32)
    wbd[...] = jnp.zeros(wbd.shape, BF16)

    def spread(d, carry):
        block = wof[pl.ds(d, 32, stride=32), :].astype(BF16)
        for a in range(4):
            at = pl.multiple_of(d * 128 + a * 32, 32)
            wbd[pl.ds(at, 32), a * 128 : (a + 1) * 128] = block
        return carry

    lax.fori_loop(0, 32, spread, 0)
    source = lax.broadcasted_iota(jnp.int32, (512, 512), 0)
    target = ((source >> 5) & 3) * 128 + (source >> 7) * 32 + (source & 31)
    column = lax.broadcasted_iota(jnp.int32, (512, 512), 1)
    perm[...] = jnp.where(column == target, 1.0, 0.0).astype(BF16)

    core = lax.rem(c, 2)

    def relay(q):
        arrived(lb.at[pl.ds(0, 2)], r_h.at[q])
        mine = lb.at[pl.ds(q * 16 + core * 8 + lax.rem(c, 8) // 2 * 2, 2)]

        def pass_on(j, carry):
            col = c // 8 * 8 + lax.rem(c + 2 * j, 8)
            remote(mine, mine, s_l, r_l.at[q], r, col).start()
            return carry

        lax.fori_loop(1, 4, pass_on, 0)

    def send_gated(q):
        def send_b(j, carry):
            row = lax.rem(r + j, ROWS)
            remote(gt.at[q, row], gb.at[r * OWN + q], s_b, r_b, row, c).start()
            return carry

        lax.fori_loop(1, ROWS, send_b, 0)
        pltpu.make_async_copy(gt.at[q, r], gb.at[r * OWN + q], r_b).start()

    def share(q):
        arrived(lb.at[pl.ds(0, 6)], r_l.at[q])
        mine = lb.at[pl.ds(q * 16 + core * 8, 8)]
        remote(mine, mine, s_c, r_c.at[q], r, c + 1 - 2 * core).start()

    def attend(q, carry):
        arrived(g.at[q], r_a.at[q])

        @pl.when(q < OWN - 1)
        def _():
            send_normed(q + 1)

        @pl.when(q == 0)
        def _():
            lax.fori_loop(1, ROWS, send_sig, 0)
            pltpu.make_async_copy(sig, sg.at[r], r_sig).start()

        column = g[q].reshape(ALL, FEAT)
        qs[...] = (dot(column, wq_ref[...]) * (32 ** (-0.5) * LOG2E)).astype(BF16)
        kt[...] = dot(column, wx_ref[:, 0:256]).T.astype(BF16)
        vs[...] = dot(column, wx_ref[:, 256:512]).astype(BF16)
        ga[...] = jax.nn.sigmoid(dot(column, wx_ref[:, 512:768]))
        for tile in range(2):
            cols = slice(tile * 128, tile * 128 + 128)
            masks = [head_mask(128, h) for h in range(4)]
            values = jnp.concatenate(
                [
                    jnp.concatenate(
                        [vs[:, cols] * mask, jnp.broadcast_to(mask, (ALL, 128))], axis=1
                    )
                    for mask in masks
                ]
            )
            for part in range(2):
                rows = slice(part * 256, part * 256 + 256)
                weights = []
                for h in range(4):
                    scores = dot(qs[rows, :] * head_mask(256, tile * 4 + h), kt[...])
                    best = jnp.max(scores, axis=-1, keepdims=True)
                    weights.append(jnp.exp2(scores - best).astype(BF16))
                found = dot(jnp.concatenate(weights, axis=1), values)
                gated = (found[:, :128] / found[:, 128:] * ga[rows, cols]).astype(BF16)
                gt[q, part * 4 : part * 4 + 4, :, cols] = gated.reshape(4, SEQ, 128)

        @pl.when(q == 0)
        def _():
            arrived(sg, r_sig)

        for part in range(2):
            rows = slice(part * 256, part * 256 + 256)
            gated = gt[q, part * 4 : part * 4 + 4].reshape(256, FEAT)
            normed = g[q, part * 4 : part * 4 + 4].reshape(256, FEAT).astype(F32)
            spreads = sg[part * 4 : part * 4 + 4].reshape(256, 128).astype(F32)
            n = r * OWN + q
            here = jnp.logical_or(lane(128) == n, lane(128) == n + RES)
            sd = jnp.sum(jnp.where(here, spreads, 0.0), axis=-1, keepdims=True)
            fresh = normed + dot(gated, wf_ref[...]) * (1.0 / sd)
            fresh = fresh - jnp.mean(fresh, axis=-1, keepdims=True)
            var = jnp.mean(fresh * fresh, axis=-1, keepdims=True)
            fresh = (fresh * (sd * lax.rsqrt(sd * sd * var + EPS))).astype(BF16)
            lrs[q, :, rows] = dot_nt(we_ref[...], fresh).astype(BF16)

        spot = q * 16 + lax.rem(r, 2) * 8 + r // 2 * 2 + lax.rem(c, 2)
        for half in range(2):
            here = jnp.logical_and(rho == r, c == half * 8 + r)

            @pl.when(here)
            def _():
                pltpu.make_async_copy(lrs.at[q, pl.ds(0, 32)], lb.at[spot], r_h.at[q]).start()

            @pl.when(jnp.logical_not(here))
            def _():
                remote(
                    lrs.at[q, pl.ds(0, 32)], lb.at[spot], s_h, r_h.at[q], rho, half * 8 + r
                ).start()

        def send_r(j, carry):
            row = lax.rem(r + j, ROWS)
            remote(
                lrs.at[q, pl.ds(32, 32)], rb.at[r * OWN + q], s_r, r_r.at[q], row, c
            ).start()
            return carry

        lax.fori_loop(1, ROWS, send_r, 0)
        pltpu.make_async_copy(lrs.at[q, pl.ds(32, 32)], rb.at[r * OWN + q], r_r.at[q]).start()
        @pl.when(q > 0)
        def _():
            relay(q - 1)

        @pl.when(q > 1)
        def _():
            share(q - 2)

        return carry

    lax.fori_loop(0, OWN, attend, 0)

    def by_channel(row, q):
        n = row * OWN + q
        for k in range(4):
            rf[k, pl.ds(n, 32, stride=32), :] = rb[n, :, k * 128 : k * 128 + 128].astype(F32)
        return q

    for q in range(OWN):
        if q == OWN - 1:
            relay(OWN - 1)
            share(OWN - 2)
        arrived(rb.at[pl.ds(0, ROWS)], r_r.at[q])
        lax.fori_loop(0, ROWS, by_channel, q, unroll=2)
    for k in range(4):
        rp[:, k * 128 : k * 128 + 128] = rf[k].astype(BF16)

    for q in range(OWN):
        send_gated(q)

    def outer(b, carry):
        left = lb[pl.ds(b * 8, 8)].reshape(256, ALL)
        for d in range(0, 32, 8):
            block = dot_nt(rp[d * 32 : d * 32 + 256, :], left) * (1.0 / ALL)
            block = block.astype(BF16)
            for e in range(8):
                for half in range(2):
                    at = pl.multiple_of(b * 64 + half * 32, 32)
                    om[pl.ds(at, 32), (d + e) * 128 : (d + e + 1) * 128] = block[
                        e * 32 : e * 32 + 32, half * 128 : half * 128 + 128
                    ]
        return carry

    def mid(b):
        update = dot(om[b * 256 : b * 256 + 256, :], wbd[...])
        for f in range(8):
            for a in range(4):
                e, q = f % 4, b * 2 + f // 4
                i = a % 2 * 32 + (e % 2 * 4 + a // 2 * 2 + e // 2) * 4 + q
                pm[q * 16 + e * 4 + a] = (
                    coup_ref[i] + update[f * 32 : f * 32 + 32, a * 128 : a * 128 + 128]
                )

    def entry(b, carry):
        pair = pm[pl.ds(b * 8, 8)].reshape(256, C_Z)
        pair = pair - jnp.mean(pair, axis=-1, keepdims=True)
        var = jnp.mean(pair * pair, axis=-1, keepdims=True)
        pair = (pair * lax.rsqrt(var + EPS)).astype(BF16)
        gp[pl.ds(b * 8, 8)] = jax.nn.sigmoid(dot(pair, wsw_ref[...])).reshape(8, RES, C_Z)
        entries = dot_nt(wit[...], pair)
        left = jax.nn.sigmoid(entries[128:256]) * entries[0:128]
        right = jax.nn.sigmoid(entries[384:512]) * entries[256:384]
        for half in range(2):
            lanes = slice(half * 128, half * 128 + 128)
            t = lax.rem(b, 4) * 2 + half
            cf[b // 4, pl.ds(t, 128, stride=16), :] = left[:, lanes]
            cf[b // 4, pl.ds(t + 8, 128, stride=16), :] = right[:, lanes]
        return carry

    corner = r * 4 + c // 4
    lanes_at = pl.multiple_of(lax.rem(c, 4) * 128, 128)

    def pairs(half):
        for q in (half * 2, half * 2 + 1):
            arrived(lb.at[pl.ds(0, 8)], r_c.at[q])
            lax.fori_loop(q * 2, q * 2 + 2, outer, 0)
            if q == OWN - 2:
                share(OWN - 1)
        mid(half)
        lax.fori_loop(half * 4, half * 4 + 4, entry, 0)

    def deal_out(half):
        cb[half] = cf[half].astype(BF16).reshape(DEVICES, 16, 128)

        def send_d(d, carry):
            peer = lax.rem(me + d, DEVICES)
            remote(
                cb.at[half, peer], xlr.at[half, corner, :, pl.ds(lanes_at, 128)],
                s_d.at[half], r_d.at[half], peer // COLS, lax.rem(peer, COLS),
            ).start()
            return carry

        lax.fori_loop(1, DEVICES, send_d, 0)
        pltpu.make_async_copy(
            cb.at[half, me], xlr.at[half, corner, :, pl.ds(lanes_at, 128)], r_d.at[half]
        ).start()

    pairs(0)
    deal_out(0)
    pairs(1)
    deal_out(1)

    arrived(gb, r_b)

    def refresh(b, carry):
        change = dot(gb[pl.ds(b * 4, 4)].reshape(256, FEAT), wf_ref[...])
        for e in range(4):
            where = pl.ds(b * 4 + e, SEQ, stride=RES)
            for k in range(2):
                xs[k, where, :] = (
                    xs[k, where, :] + change[e * 64 : e * 64 + 64, k * 128 : k * 128 + 128]
                )
        return carry

    lax.fori_loop(0, RES // 4, refresh, 0)
    store = [
        pltpu.make_async_copy(xs.at[k], out_m.at[:, pl.ds(k * 128, 128)], s_x.at[k])
        for k in range(2)
    ]
    store[0].start()
    store[1].start()

    def line_up(b, half):
        moved = dot(xlr[half, pl.ds(b * 8, 8)].reshape(128, 512), perm[...])
        for e in range(4):
            for a in range(4):
                at = pl.multiple_of(half * 256 + b * 64 + a * 16, 16)
                lanes = slice(a * 128, a * 128 + 128)
                spot = slice(e * 128, e * 128 + 128)
                one, two = moved[e * 16 : e * 16 + 16, lanes], moved[e * 16 + 64 : e * 16 + 80, lanes]
                am[pl.ds(at, 16), spot] = jnp.concatenate([one[:8], two[:8]]).astype(BF16)
                bm[pl.ds(at, 16), spot] = jnp.concatenate([one[8:], two[8:]]).astype(BF16)
        return half

    arrived(xlr.at[0], r_d.at[0])
    lax.fori_loop(0, 4, line_up, 0)
    pa[...] = dot_tn(am[0:256, :], bm[0:256, :])
    arrived(xlr.at[1], r_d.at[1])
    lax.fori_loop(0, 4, line_up, 1)
    pb[...] = (pa[...] + dot_tn(am[256:512, :], bm[256:512, :])).astype(BF16)

    def deal(b, carry):
        row = lax.rem(r + b, ROWS)
        for e in range(4):
            for a in range(4):
                at = pl.multiple_of(row * 64 + a * 16, 16)
                xe[e * 16 : e * 16 + 16, a * 128 : a * 128 + 128] = pb[
                    pl.ds(at, 16), e * 128 : e * 128 + 128
                ]
        es[pl.ds(row * 4, 4)] = dot(xe[...], perm[...]).astype(BF16).reshape(4, 16, 512)

        def piece(col):
            at = pl.multiple_of(lax.rem(col, 4) * 128, 128)
            return es.at[row * 4 + col // 4, :, pl.ds(at, 128)]

        def send_e(j, inner):
            col = lax.rem(c + j, COLS)
            remote(piece(col), er.at[me], s_e, r_e, row, col).start()
            return inner

        lax.fori_loop(1, COLS, send_e, 0)

        @pl.when(b == 0)
        def _():
            pltpu.make_async_copy(piece(c), er.at[me], r_e).start()

        @pl.when(b > 0)
        def _():
            remote(piece(c), er.at[me], s_e, r_e, row, c).start()

        return carry

    lax.fori_loop(0, ROWS, deal, 0)
    arrived(er, r_e)

    ef[...] = er[...].astype(F32).reshape(DEVICES * 16, 128)

    def final(t, carry):
        prod = ef[pl.ds(t, DEVICES, stride=16), :]
        prod = prod - jnp.mean(prod, axis=0, keepdims=True)
        var = jnp.mean(prod * prod, axis=0, keepdims=True)
        prod = (prod * lax.rsqrt(var + EPS)).astype(BF16)
        update = dot_tn(prod, wtri_ref[...])
        for a in range(4):
            p = lax.rem(t, 4) * 16 + lax.rem(t // 4, 2) * 8 + (a % 2 * 2 + t // 8) * 2 + a // 2
            out_p[a * 16 + t] = pm[p] + gp[p] * update[a * 32 : a * 32 + 32]
        return carry

    lax.fori_loop(0, 16, final, 0, unroll=4)

    store[0].wait()
    store[1].wait()
    for q in range(OWN):
        arrived(nt.at[q, pl.ds(0, 7)], s_a.at[q])
    arrived(sg.at[pl.ds(0, 7)], s_sig)
    arrived(gb.at[pl.ds(0, 28)], s_b)
    arrived(rb.at[pl.ds(0, 28)], s_r)

    relays_itself = jnp.logical_and(rho == r, lax.rem(c, 8) == r)

    @pl.when(relays_itself)
    def _():
        arrived(lb.at[pl.ds(0, 4)], s_h)

    @pl.when(jnp.logical_not(relays_itself))
    def _():
        arrived(lb.at[pl.ds(0, 8)], s_h)

    arrived(lb.at[pl.ds(0, 24)], s_l)
    arrived(lb.at[pl.ds(0, 32)], s_c)
    for half in range(2):
        arrived(cb.at[half, pl.ds(0, DEVICES - 1)], s_d.at[half])
    arrived(er.at[pl.ds(0, DEVICES - 1)], s_e)


def body(x, coup, wq, wx, wf, we, wo, wi, wsw, wtri):
    vmem = pl.BlockSpec(memory_space=pltpu.VMEM)
    hbm = pl.BlockSpec(memory_space=pl.ANY)
    dma = pltpu.SemaphoreType.DMA
    out_m, out_p = pl.pallas_call(
        kernel,
        out_shape=(
            jax.ShapeDtypeStruct((SEQ * RES, FEAT), F32),
            jax.ShapeDtypeStruct((SEQ, RES, C_Z), F32),
        ),
        in_specs=[hbm] + [vmem] * 9,
        out_specs=(hbm, vmem),
        scratch_shapes=[
            pltpu.VMEM((2, SEQ * RES, 128), F32),
            pltpu.VMEM((OWN, ROWS, SEQ, FEAT), BF16),
            pltpu.VMEM((OWN, ROWS, SEQ, FEAT), BF16),
            pltpu.VMEM((SEQ, 128), BF16),
            pltpu.VMEM((ROWS, SEQ, 128), BF16),
            pltpu.VMEM((ALL, FEAT), BF16),
            pltpu.VMEM((FEAT, ALL), BF16),
            pltpu.VMEM((ALL, FEAT), BF16),
            pltpu.VMEM((ALL, FEAT), F32),
            pltpu.VMEM((OWN, ROWS, SEQ, FEAT), BF16),
            pltpu.VMEM((RES, SEQ, FEAT), BF16),
            pltpu.VMEM((OWN, 64, ALL), BF16),
            pltpu.VMEM((RES, 32, ALL), BF16),
            pltpu.VMEM((SEQ, 32, ALL), BF16),
            pltpu.VMEM((512, C_Z), BF16),
            pltpu.VMEM((1024, C_Z), F32),
            pltpu.VMEM((4096, 512), BF16),
            pltpu.VMEM((512, 512), BF16),
            pltpu.VMEM((4, 1024, 128), F32),
            pltpu.VMEM((1024, ALL), BF16),
            pltpu.VMEM((512, 4096), BF16),
            pltpu.VMEM((SEQ, RES, C_Z), F32),
            pltpu.VMEM((SEQ, RES, C_Z), F32),
            pltpu.VMEM((2, DEVICES * 16, 128), F32),
            pltpu.VMEM((2, DEVICES, 16, 128), BF16),
            pltpu.VMEM((2, 32, 16, 512), BF16),
            pltpu.VMEM((512, 512), BF16),
            pltpu.VMEM((512, 512), BF16),
            pltpu.VMEM((512, 512), F32),
            pltpu.VMEM((512, 512), BF16),
            pltpu.VMEM((64, 512), BF16),
            pltpu.VMEM((32, 16, 512), BF16),
            pltpu.VMEM((DEVICES, 16, 128), BF16),
            pltpu.VMEM((DEVICES * 16, 128), F32),
            dma((2,)),
            dma((OWN,)), dma((OWN,)),
            dma(()), dma(()),
            dma(()), dma(()),
            dma(()), dma((OWN,)),
            dma(()), dma((OWN,)),
            dma(()), dma((OWN,)),
            dma(()), dma((OWN,)),
            dma((2,)), dma((2,)),
            dma(()), dma(()),
        ],
        compiler_params=pltpu.CompilerParams(
            collective_id=0, has_side_effects=True, vmem_limit_bytes=56 * 2**20
        ),
    )(x.reshape(SEQ * RES, FEAT), coup, wq, wx, wf, we.T, wo, wi, wsw, wtri)
    return out_m.reshape(SEQ, RES, FEAT), out_p


def solution(mesh):
    spread = P("row", "col", None)
    return jax.shard_map(
        body, mesh=mesh, in_specs=(spread, spread) + (P(),) * 8,
        out_specs=(spread, spread), check_vma=False,
    )
```

```python
import functools

import jax
import jax.numpy as jnp
from jax import lax
from jax.experimental import pallas as pl
from jax.experimental.pallas import tpu as pltpu
from jax.sharding import PartitionSpec as P

F32, BF16 = jnp.float32, jnp.bfloat16
MESH = pl.DeviceIdType.MESH
EPS = 1e-05
LOG2E = 1.4426950408889634
ROWS, COLS = 8, 16
DEVICES = ROWS * COLS
SEQ, RES = 64, 32
OWN = 4
ALL = 512
FEAT, HEADS = 256, 8
C_Z = 128


def dot(a, b):
    return jnp.dot(a, b, preferred_element_type=F32)


def dot_nt(a, b):
    return lax.dot_general(a, b, (((1,), (1,)), ((), ())), preferred_element_type=F32)


def dot_tn(a, b):
    return lax.dot_general(a, b, (((0,), (0,)), ((), ())), preferred_element_type=F32)


def lane(width):
    return lax.broadcasted_iota(jnp.int32, (1, width), 1)


def head_mask(width, which):
    return jnp.where((lane(width) >> 5) == which, 1.0, 0.0).astype(BF16)


def kernel(
    x_ref, coup_ref, wq_ref, wx_ref, wf_ref, we_ref, wo_ref, wi_ref, wsw_ref, wtri_ref,
    out_m, out_p,
    xs, coup, nt, g, sig, sg, qs, kt, vs, ga, gt, gb, lrs, rb, lb,
    wit, wof, wbd, perm, rf, rp, om, pm, gp, cf, cb, xlr, am, bm, pa, pb, xe, es, er, ef,
    everyone, s_x, s_c0, s_a, r_a, s_sig, r_sig, s_b, r_b, s_h, r_h, s_t, r_t, s_l, r_l, s_c, r_c, s_r, r_r, s_d, r_d, s_e, r_e,
):
    r = lax.axis_index("row")
    c = lax.axis_index("col")
    me = r * COLS + c
    rho = c // 2

    def remote(src, dst, send, recv, row, col):
        return pltpu.make_async_remote_copy(
            src_ref=src, dst_ref=dst, send_sem=send, recv_sem=recv,
            device_id=(row, col), device_id_type=MESH,
        )

    def arrived(ref, sem):
        pltpu.make_async_copy(ref, ref, sem).wait()

    load = [
        pltpu.make_async_copy(x_ref.at[:, pl.ds(k * 128, 128)], xs.at[k], s_x.at[k])
        for k in range(2)
    ]
    load[0].start()
    load[1].start()
    couplings = pltpu.make_async_copy(coup_ref, coup, s_c0)

    barrier = pltpu.get_barrier_semaphore()

    def greet_along_row(d, carry):
        pl.semaphore_signal(
            barrier, inc=1, device_id=(lax.rem(r + d, ROWS), c), device_id_type=MESH
        )
        return carry

    def greet_along_col(d, carry):
        pl.semaphore_signal(
            barrier, inc=1, device_id=(r, lax.rem(c + d, COLS)), device_id_type=MESH
        )
        return carry

    lax.fori_loop(1, ROWS, greet_along_row, 0)
    lax.fori_loop(1, COLS, greet_along_col, 0)

    def tell(d, carry):
        pl.semaphore_signal(
            everyone, inc=1, device_id=(r, lax.rem(c + d, COLS)), device_id_type=MESH
        )
        return carry

    def norm_one(q, row, stats):
        n = row * OWN + q
        x0 = xs[0, pl.ds(n, SEQ, stride=RES), :]
        x1 = xs[1, pl.ds(n, SEQ, stride=RES), :]
        mean = jnp.sum(x0 + x1, axis=-1, keepdims=True) * (1.0 / FEAT)
        x0, x1 = x0 - mean, x1 - mean
        var = jnp.sum(x0 * x0 + x1 * x1, axis=-1, keepdims=True) * (1.0 / FEAT) + EPS
        inv = lax.rsqrt(var)
        nt[q, row, :, 0:128] = (x0 * inv).astype(BF16)
        nt[q, row, :, 128:256] = (x1 * inv).astype(BF16)
        sd = var * inv
        high = sd.astype(BF16).astype(F32)
        stats = jnp.where(lane(128) == n, high, stats)
        return jnp.where(lane(128) == n + RES, sd - high, stats)

    load[0].wait()
    load[1].wait()
    def send_normed(q):
        def send_a(j, carry):
            row = lax.rem(r + j, ROWS)
            remote(nt.at[q, row], g.at[q, r], s_a.at[q], r_a.at[q], row, c).start()
            return carry

        lax.fori_loop(1, ROWS, send_a, 0)
        pltpu.make_async_copy(nt.at[q, r], g.at[q, r], r_a.at[q]).start()

    def send_sig(j, carry):
        row = lax.rem(r + j, ROWS)
        remote(sig, sg.at[r], s_sig, r_sig, row, c).start()
        return carry

    stats = jnp.zeros((SEQ, 128), F32)
    for q in range(OWN):
        stats = lax.fori_loop(0, ROWS, lambda row, s, q=q: norm_one(q, row, s), stats, unroll=4)
        if q == 0:
            pl.semaphore_wait(barrier, ROWS - 1 + COLS - 1)
            send_normed(0)
            lax.fori_loop(1, COLS, tell, 0)
        if q == 1:
            send_normed(1)
    sig[...] = stats.astype(BF16)
    couplings.start()

    wit[...] = wi_ref[...].astype(F32).T.astype(BF16)
    wof[...] = wo_ref[...].astype(F32)
    wbd[...] = jnp.zeros(wbd.shape, BF16)

    def spread(d, carry):
        block = wof[pl.ds(d, 32, stride=32), :].astype(BF16)
        for a in range(4):
            at = pl.multiple_of(d * 128 + a * 32, 32)
            wbd[pl.ds(at, 32), a * 128 : (a + 1) * 128] = block
        return carry

    lax.fori_loop(0, 32, spread, 0)
    source = lax.broadcasted_iota(jnp.int32, (512, 512), 0)
    target = ((source >> 5) & 3) * 128 + (source >> 7) * 32 + (source & 31)
    column = lax.broadcasted_iota(jnp.int32, (512, 512), 1)
    perm[...] = jnp.where(column == target, 1.0, 0.0).astype(BF16)

    core = lax.rem(c, 2)

    def slot(q, half):
        return lb.at[q * 16 + core * 8 + lax.rem(c, 8) // 2 * 2 + half]

    def pass_on(q, half):
        def send_l(j, carry):
            col = c // 8 * 8 + lax.rem(c + 2 * j, 8)
            remote(slot(q, half), slot(q, half), s_l, r_l.at[q], r, col).start()
            return carry

        lax.fori_loop(1, 4, send_l, 0)

    def relay(q):
        arrived(lb.at[0], r_h.at[q])
        mine = slot(q, c // 8)
        remote(mine, mine, s_t, r_t.at[q], r, lax.rem(c + 8, COLS)).start()
        pass_on(q, c // 8)

    def relay_twin(q):
        arrived(lb.at[0], r_t.at[q])
        pass_on(q, 1 - c // 8)

    def send_gated(q):
        def send_b(j, carry):
            row = lax.rem(r + j, ROWS)
            remote(gt.at[q, row], gb.at[r * OWN + q], s_b, r_b, row, c).start()
            return carry

        lax.fori_loop(1, ROWS, send_b, 0)
        pltpu.make_async_copy(gt.at[q, r], gb.at[r * OWN + q], r_b).start()

    def share(q):
        arrived(lb.at[pl.ds(0, 6)], r_l.at[q])
        mine = lb.at[pl.ds(q * 16 + core * 8, 8)]
        remote(mine, mine, s_c, r_c.at[q], r, c + 1 - 2 * core).start()

    def attend(q, carry):
        arrived(g.at[q], r_a.at[q])

        @pl.when(q < OWN - 2)
        def _():
            send_normed(q + 2)

        @pl.when(q == 0)
        def _():
            lax.fori_loop(1, ROWS, send_sig, 0)
            pltpu.make_async_copy(sig, sg.at[r], r_sig).start()

        column = g[q].reshape(ALL, FEAT)
        qs[...] = (dot(column, wq_ref[...]) * (32 ** (-0.5) * LOG2E)).astype(BF16)
        kt[...] = dot(column, wx_ref[:, 0:256]).T.astype(BF16)
        vs[...] = dot(column, wx_ref[:, 256:512]).astype(BF16)
        ga[...] = jax.nn.sigmoid(dot(column, wx_ref[:, 512:768]))
        for tile in range(2):
            cols = slice(tile * 128, tile * 128 + 128)
            masks = [head_mask(128, h) for h in range(4)]
            values = jnp.concatenate(
                [
                    jnp.concatenate(
                        [vs[:, cols] * mask, jnp.broadcast_to(mask, (ALL, 128))], axis=1
                    )
                    for mask in masks
                ]
            )
            for part in range(2):
                rows = slice(part * 256, part * 256 + 256)
                weights = []
                for h in range(4):
                    scores = dot(qs[rows, :] * head_mask(256, tile * 4 + h), kt[...])
                    best = jnp.max(scores, axis=-1, keepdims=True)
                    weights.append(jnp.exp2(scores - best).astype(BF16))
                found = dot(jnp.concatenate(weights, axis=1), values)
                gated = (found[:, :128] / found[:, 128:] * ga[rows, cols]).astype(BF16)
                gt[q, part * 4 : part * 4 + 4, :, cols] = gated.reshape(4, SEQ, 128)

        @pl.when(q == 0)
        def _():
            arrived(sg, r_sig)
            pl.semaphore_wait(everyone, COLS - 1)

        for part in range(2):
            rows = slice(part * 256, part * 256 + 256)
            gated = gt[q, part * 4 : part * 4 + 4].reshape(256, FEAT)
            normed = g[q, part * 4 : part * 4 + 4].reshape(256, FEAT).astype(F32)
            spreads = sg[part * 4 : part * 4 + 4].reshape(256, 128).astype(F32)
            n = r * OWN + q
            here = jnp.logical_or(lane(128) == n, lane(128) == n + RES)
            sd = jnp.sum(jnp.where(here, spreads, 0.0), axis=-1, keepdims=True)
            fresh = normed + dot(gated, wf_ref[...]) * (1.0 / sd)
            fresh = fresh - jnp.mean(fresh, axis=-1, keepdims=True)
            var = jnp.mean(fresh * fresh, axis=-1, keepdims=True)
            fresh = (fresh * (sd * lax.rsqrt(sd * sd * var + EPS))).astype(BF16)
            lrs[q, :, rows] = dot_nt(we_ref[...], fresh).astype(BF16)

        spot = q * 16 + lax.rem(r, 2) * 8 + r // 2 * 2 + lax.rem(c, 2)
        meet = lax.rem(c, 2) * 8 + r
        here = jnp.logical_and(rho == r, c == meet)

        @pl.when(here)
        def _():
            pltpu.make_async_copy(lrs.at[q, pl.ds(0, 32)], lb.at[spot], r_h.at[q]).start()

        @pl.when(jnp.logical_not(here))
        def _():
            remote(lrs.at[q, pl.ds(0, 32)], lb.at[spot], s_h, r_h.at[q], rho, meet).start()

        def send_r(j, carry):
            row = lax.rem(r + j, ROWS)
            remote(
                lrs.at[q, pl.ds(32, 32)], rb.at[r * OWN + q], s_r, r_r.at[q], row, c
            ).start()
            return carry

        lax.fori_loop(1, ROWS, send_r, 0)
        pltpu.make_async_copy(lrs.at[q, pl.ds(32, 32)], rb.at[r * OWN + q], r_r.at[q]).start()
        @pl.when(q > 0)
        def _():
            relay(q - 1)

        @pl.when(q > 1)
        def _():
            relay_twin(q - 2)

        @pl.when(q > 2)
        def _():
            share(q - 3)

        return carry

    lax.fori_loop(0, OWN, attend, 0)

    def by_channel(row, q):
        n = row * OWN + q
        for k in range(4):
            rf[k, pl.ds(n, 32, stride=32), :] = rb[n, :, k * 128 : k * 128 + 128].astype(F32)
        return q

    for q in range(OWN):
        if q == OWN - 1:
            relay_twin(OWN - 2)
            relay(OWN - 1)
            share(OWN - 3)
        arrived(rb.at[pl.ds(0, ROWS)], r_r.at[q])
        lax.fori_loop(0, ROWS, by_channel, q, unroll=2)
    for k in range(4):
        rp[:, k * 128 : k * 128 + 128] = rf[k].astype(BF16)

    for q in range(OWN):
        send_gated(q)

    def outer(b, carry):
        left = lb[pl.ds(b * 8, 8)].reshape(256, ALL)
        for d in range(0, 32, 8):
            block = dot_nt(rp[d * 32 : d * 32 + 256, :], left) * (1.0 / ALL)
            block = block.astype(BF16)
            for e in range(8):
                for half in range(2):
                    at = pl.multiple_of(b * 64 + half * 32, 32)
                    om[pl.ds(at, 32), (d + e) * 128 : (d + e + 1) * 128] = block[
                        e * 32 : e * 32 + 32, half * 128 : half * 128 + 128
                    ]
        return carry

    def mid(b):
        update = dot(om[b * 256 : b * 256 + 256, :], wbd[...])
        for f in range(8):
            for a in range(4):
                e, q = f % 4, b * 2 + f // 4
                i = a % 2 * 32 + (e % 2 * 4 + a // 2 * 2 + e // 2) * 4 + q
                pm[q * 16 + e * 4 + a] = (
                    coup[i] + update[f * 32 : f * 32 + 32, a * 128 : a * 128 + 128]
                )

    def entry(b, carry):
        pair = pm[pl.ds(b * 8, 8)].reshape(256, C_Z)
        pair = pair - jnp.mean(pair, axis=-1, keepdims=True)
        var = jnp.mean(pair * pair, axis=-1, keepdims=True)
        pair = (pair * lax.rsqrt(var + EPS)).astype(BF16)
        gp[pl.ds(b * 8, 8)] = jax.nn.sigmoid(dot(pair, wsw_ref[...])).reshape(8, RES, C_Z)
        entries = dot_nt(wit[...], pair)
        left = jax.nn.sigmoid(entries[128:256]) * entries[0:128]
        right = jax.nn.sigmoid(entries[384:512]) * entries[256:384]
        for half in range(2):
            lanes = slice(half * 128, half * 128 + 128)
            t = lax.rem(b, 4) * 2 + half
            cf[b // 4, pl.ds(t, 128, stride=16), :] = left[:, lanes]
            cf[b // 4, pl.ds(t + 8, 128, stride=16), :] = right[:, lanes]
        return carry

    corner = r * 4 + c // 4
    lanes_at = pl.multiple_of(lax.rem(c, 4) * 128, 128)

    def pairs(half):
        for q in (half * 2, half * 2 + 1):
            arrived(lb.at[pl.ds(0, 8)], r_c.at[q])
            lax.fori_loop(q * 2, q * 2 + 2, outer, 0)
            if q == 0:
                relay_twin(OWN - 1)
                share(OWN - 2)
        mid(half)
        lax.fori_loop(half * 4, half * 4 + 4, entry, 0)

    def deal_out(half):
        cb[half] = cf[half].astype(BF16).reshape(DEVICES, 16, 128)

        def send_d(d, carry):
            peer = lax.rem(me + d, DEVICES)
            remote(
                cb.at[half, peer], xlr.at[half, corner, :, pl.ds(lanes_at, 128)],
                s_d.at[half], r_d.at[half], peer // COLS, lax.rem(peer, COLS),
            ).start()
            return carry

        lax.fori_loop(1, DEVICES, send_d, 0)
        pltpu.make_async_copy(
            cb.at[half, me], xlr.at[half, corner, :, pl.ds(lanes_at, 128)], r_d.at[half]
        ).start()

    couplings.wait()
    pairs(0)
    share(OWN - 1)
    deal_out(0)
    pairs(1)
    deal_out(1)

    arrived(gb, r_b)

    def refresh(b, carry):
        change = dot(gb[pl.ds(b * 4, 4)].reshape(256, FEAT), wf_ref[...])
        for e in range(4):
            where = pl.ds(b * 4 + e, SEQ, stride=RES)
            for k in range(2):
                xs[k, where, :] = (
                    xs[k, where, :] + change[e * 64 : e * 64 + 64, k * 128 : k * 128 + 128]
                )
        return carry

    lax.fori_loop(0, RES // 4, refresh, 0)
    store = [
        pltpu.make_async_copy(xs.at[k], out_m.at[:, pl.ds(k * 128, 128)], s_x.at[k])
        for k in range(2)
    ]
    store[0].start()
    store[1].start()

    def line_up(b, half):
        moved = dot(xlr[half, pl.ds(b * 8, 8)].reshape(128, 512), perm[...])
        for e in range(4):
            for a in range(4):
                at = pl.multiple_of(half * 256 + b * 64 + a * 16, 16)
                lanes = slice(a * 128, a * 128 + 128)
                spot = slice(e * 128, e * 128 + 128)
                one, two = moved[e * 16 : e * 16 + 16, lanes], moved[e * 16 + 64 : e * 16 + 80, lanes]
                am[pl.ds(at, 16), spot] = jnp.concatenate([one[:8], two[:8]]).astype(BF16)
                bm[pl.ds(at, 16), spot] = jnp.concatenate([one[8:], two[8:]]).astype(BF16)
        return half

    arrived(xlr.at[0], r_d.at[0])
    lax.fori_loop(0, 4, line_up, 0)
    pa[...] = dot_tn(am[0:256, :], bm[0:256, :])
    arrived(xlr.at[1], r_d.at[1])
    lax.fori_loop(0, 4, line_up, 1)
    pb[...] = (pa[...] + dot_tn(am[256:512, :], bm[256:512, :])).astype(BF16)

    def deal(b, carry):
        row = lax.rem(r + b, ROWS)
        for e in range(4):
            for a in range(4):
                at = pl.multiple_of(row * 64 + a * 16, 16)
                xe[e * 16 : e * 16 + 16, a * 128 : a * 128 + 128] = pb[
                    pl.ds(at, 16), e * 128 : e * 128 + 128
                ]
        es[pl.ds(row * 4, 4)] = dot(xe[...], perm[...]).astype(BF16).reshape(4, 16, 512)

        def piece(col):
            at = pl.multiple_of(lax.rem(col, 4) * 128, 128)
            return es.at[row * 4 + col // 4, :, pl.ds(at, 128)]

        def send_e(j, inner):
            col = lax.rem(c + j, COLS)
            remote(piece(col), er.at[me], s_e, r_e, row, col).start()
            return inner

        lax.fori_loop(1, COLS, send_e, 0)

        @pl.when(b == 0)
        def _():
            pltpu.make_async_copy(piece(c), er.at[me], r_e).start()

        @pl.when(b > 0)
        def _():
            remote(piece(c), er.at[me], s_e, r_e, row, c).start()

        return carry

    lax.fori_loop(0, ROWS, deal, 0)
    arrived(er, r_e)

    ef[...] = er[...].astype(F32).reshape(DEVICES * 16, 128)

    def final(t, carry):
        prod = ef[pl.ds(t, DEVICES, stride=16), :]
        prod = prod - jnp.mean(prod, axis=0, keepdims=True)
        var = jnp.mean(prod * prod, axis=0, keepdims=True)
        prod = (prod * lax.rsqrt(var + EPS)).astype(BF16)
        update = dot_tn(prod, wtri_ref[...])
        for a in range(4):
            p = lax.rem(t, 4) * 16 + lax.rem(t // 4, 2) * 8 + (a % 2 * 2 + t // 8) * 2 + a // 2
            out_p[a * 16 + t] = pm[p] + gp[p] * update[a * 32 : a * 32 + 32]
        return carry

    lax.fori_loop(0, 16, final, 0, unroll=4)

    store[0].wait()
    store[1].wait()
    for q in range(OWN):
        arrived(nt.at[q, pl.ds(0, 7)], s_a.at[q])
    arrived(sg.at[pl.ds(0, 7)], s_sig)
    arrived(gb.at[pl.ds(0, 28)], s_b)
    arrived(rb.at[pl.ds(0, 28)], s_r)


    @pl.when(jnp.logical_not(jnp.logical_and(rho == r, lax.rem(c, 2) * 8 + r == c)))
    def _():
        arrived(lb.at[pl.ds(0, OWN)], s_h)

    arrived(lb.at[pl.ds(0, OWN)], s_t)
    arrived(lb.at[pl.ds(0, 24)], s_l)
    arrived(lb.at[pl.ds(0, 32)], s_c)
    for half in range(2):
        arrived(cb.at[half, pl.ds(0, DEVICES - 1)], s_d.at[half])
    arrived(er.at[pl.ds(0, DEVICES - 1)], s_e)


def hand_over(m_ref, p_ref, out_m, out_p, m, p, sems):
    def pieces(source, held, result, count, first):
        rows = held.shape[0] // count
        for k in range(count):
            at = pl.ds(k * rows, rows)
            yield (
                pltpu.make_async_copy(source.at[at], held.at[at], sems.at[first + k]),
                pltpu.make_async_copy(held.at[at], result.at[at], sems.at[first + k]),
            )

    copies = list(pieces(m_ref, m, out_m, 8, 0)) + list(pieces(p_ref, p, out_p, 4, 8))
    for load, _ in copies:
        load.start()
    for load, store in copies:
        load.wait()
        store.start()
    for _, store in copies:
        store.wait()


def body(x, coup, wq, wx, wf, we, wo, wi, wsw, wtri):
    vmem = pl.BlockSpec(memory_space=pltpu.VMEM)
    hbm = pl.BlockSpec(memory_space=pl.ANY)
    dma = pltpu.SemaphoreType.DMA
    out_m, out_p = pl.pallas_call(
        kernel,
        out_shape=(
            jax.ShapeDtypeStruct((SEQ * RES, FEAT), F32),
            jax.ShapeDtypeStruct((SEQ, RES, C_Z), F32),
        ),
        in_specs=[hbm] * 2 + [vmem] * 8,
        out_specs=(hbm, vmem),
        scratch_shapes=[
            pltpu.VMEM((2, SEQ * RES, 128), F32),
            pltpu.VMEM((SEQ, RES, C_Z), F32),
            pltpu.VMEM((OWN, ROWS, SEQ, FEAT), BF16),
            pltpu.VMEM((OWN, ROWS, SEQ, FEAT), BF16),
            pltpu.VMEM((SEQ, 128), BF16),
            pltpu.VMEM((ROWS, SEQ, 128), BF16),
            pltpu.VMEM((ALL, FEAT), BF16),
            pltpu.VMEM((FEAT, ALL), BF16),
            pltpu.VMEM((ALL, FEAT), BF16),
            pltpu.VMEM((ALL, FEAT), F32),
            pltpu.VMEM((OWN, ROWS, SEQ, FEAT), BF16),
            pltpu.VMEM((RES, SEQ, FEAT), BF16),
            pltpu.VMEM((OWN, 64, ALL), BF16),
            pltpu.VMEM((RES, 32, ALL), BF16),
            pltpu.VMEM((SEQ, 32, ALL), BF16),
            pltpu.VMEM((512, C_Z), BF16),
            pltpu.VMEM((1024, C_Z), F32),
            pltpu.VMEM((4096, 512), BF16),
            pltpu.VMEM((512, 512), BF16),
            pltpu.VMEM((4, 1024, 128), F32),
            pltpu.VMEM((1024, ALL), BF16),
            pltpu.VMEM((512, 4096), BF16),
            pltpu.VMEM((SEQ, RES, C_Z), F32),
            pltpu.VMEM((SEQ, RES, C_Z), F32),
            pltpu.VMEM((2, DEVICES * 16, 128), F32),
            pltpu.VMEM((2, DEVICES, 16, 128), BF16),
            pltpu.VMEM((2, 32, 16, 512), BF16),
            pltpu.VMEM((512, 512), BF16),
            pltpu.VMEM((512, 512), BF16),
            pltpu.VMEM((512, 512), F32),
            pltpu.VMEM((512, 512), BF16),
            pltpu.VMEM((64, 512), BF16),
            pltpu.VMEM((32, 16, 512), BF16),
            pltpu.VMEM((DEVICES, 16, 128), BF16),
            pltpu.VMEM((DEVICES * 16, 128), F32),
            pltpu.SemaphoreType.REGULAR,
            dma((2,)),
            dma(()),
            dma((OWN,)), dma((OWN,)),
            dma(()), dma(()),
            dma(()), dma(()),
            dma(()), dma((OWN,)),
            dma(()), dma((OWN,)),
            dma(()), dma((OWN,)),
            dma(()), dma((OWN,)),
            dma(()), dma((OWN,)),
            dma((2,)), dma((2,)),
            dma(()), dma(()),
        ],
        compiler_params=pltpu.CompilerParams(
            collective_id=0, has_side_effects=True, vmem_limit_bytes=56 * 2**20
        ),
    )(x.reshape(SEQ * RES, FEAT), coup, wq, wx, wf, we.T, wo, wi, wsw, wtri)
    out_m, out_p = pl.pallas_call(
        hand_over,
        out_shape=(
            jax.ShapeDtypeStruct((SEQ * RES, FEAT), F32),
            jax.ShapeDtypeStruct((SEQ, RES, C_Z), F32),
        ),
        in_specs=[hbm] * 2,
        out_specs=(hbm, hbm),
        scratch_shapes=[
            pltpu.VMEM((SEQ * RES, FEAT), F32), pltpu.VMEM((SEQ, RES, C_Z), F32), dma((12,)),
        ],
    )(out_m, out_p)
    return out_m.reshape(SEQ, RES, FEAT), out_p


def solution(mesh):
    spread = P("row", "col", None)
    return jax.shard_map(
        body, mesh=mesh, in_specs=(spread, spread) + (P(),) * 8,
        out_specs=(spread, spread), check_vma=False,
    )
```

```python
import functools

import jax
import jax.numpy as jnp
from jax import lax
from jax.experimental import pallas as pl
from jax.experimental.pallas import tpu as pltpu
from jax.sharding import PartitionSpec as P

F32, BF16 = jnp.float32, jnp.bfloat16
MESH = pl.DeviceIdType.MESH
EPS = 1e-05
LOG2E = 1.4426950408889634
ROWS, COLS = 8, 16
DEVICES = ROWS * COLS
SEQ, RES = 64, 32
OWN = 4
ALL = 512
FEAT, HEADS = 256, 8
C_Z = 128


def dot(a, b):
    return jnp.dot(a, b, preferred_element_type=F32)


def dot_nt(a, b):
    return lax.dot_general(a, b, (((1,), (1,)), ((), ())), preferred_element_type=F32)


def dot_tn(a, b):
    return lax.dot_general(a, b, (((0,), (0,)), ((), ())), preferred_element_type=F32)


def lane(width):
    return lax.broadcasted_iota(jnp.int32, (1, width), 1)


def head_mask(width, which):
    return jnp.where((lane(width) >> 5) == which, 1.0, 0.0).astype(BF16)


def kernel(
    x_ref, coup_ref, wq_in, wx_in, wf_in, we_in, wo_in, wi_in, wsw_in, wtri_in,
    out_m, out_p,
    wq_ref, wx_ref, wf_ref, we_ref, wo_ref, wi_ref, wsw_ref, wtri_ref,
    xs, coup, nt, g, sig, sg, qs, kt, vs, ga, gt, gb, lrs, rb, lb,
    wit, wof, wbd, perm, rf, rp, om, pm, gp, cf, cb, xlr, am, bm, pa, pb, xe, es, er, ef,
    everyone, s_x, s_c0, s_w, s_o, s_a, r_a, s_sig, r_sig, s_b, r_b, s_h, r_h, s_t, r_t, s_l, r_l, s_c, r_c, s_r, r_r, s_d, r_d, s_e, r_e,
):
    r = lax.axis_index("row")
    c = lax.axis_index("col")
    me = r * COLS + c
    rho = c // 2

    def remote(src, dst, send, recv, row, col):
        return pltpu.make_async_remote_copy(
            src_ref=src, dst_ref=dst, send_sem=send, recv_sem=recv,
            device_id=(row, col), device_id_type=MESH,
        )

    def arrived(ref, sem):
        pltpu.make_async_copy(ref, ref, sem).wait()

    load = [
        pltpu.make_async_copy(x_ref.at[:, pl.ds(k * 128, 128)], xs.at[k], s_x.at[k])
        for k in range(2)
    ]
    load[0].start()
    load[1].start()
    couplings = pltpu.make_async_copy(coup_ref, coup, s_c0)
    weights_in = [
        pltpu.make_async_copy(source, held, s_w.at[k])
        for k, (source, held) in enumerate(
            (
                (wq_in, wq_ref), (wx_in, wx_ref), (wf_in, wf_ref), (we_in, we_ref),
                (wo_in, wo_ref), (wi_in, wi_ref), (wsw_in, wsw_ref), (wtri_in, wtri_ref),
            )
        )
    ]

    barrier = pltpu.get_barrier_semaphore()

    def greet_along_row(d, carry):
        pl.semaphore_signal(
            barrier, inc=1, device_id=(lax.rem(r + d, ROWS), c), device_id_type=MESH
        )
        return carry

    def greet_along_col(d, carry):
        pl.semaphore_signal(
            barrier, inc=1, device_id=(r, lax.rem(c + d, COLS)), device_id_type=MESH
        )
        return carry

    lax.fori_loop(1, ROWS, greet_along_row, 0)
    lax.fori_loop(1, COLS, greet_along_col, 0)

    def tell(d, carry):
        pl.semaphore_signal(
            everyone, inc=1, device_id=(r, lax.rem(c + d, COLS)), device_id_type=MESH
        )
        return carry

    def norm_one(q, row, stats):
        n = row * OWN + q
        x0 = xs[0, pl.ds(n, SEQ, stride=RES), :]
        x1 = xs[1, pl.ds(n, SEQ, stride=RES), :]
        mean = jnp.sum(x0 + x1, axis=-1, keepdims=True) * (1.0 / FEAT)
        x0, x1 = x0 - mean, x1 - mean
        var = jnp.sum(x0 * x0 + x1 * x1, axis=-1, keepdims=True) * (1.0 / FEAT) + EPS
        inv = lax.rsqrt(var)
        nt[q, row, :, 0:128] = (x0 * inv).astype(BF16)
        nt[q, row, :, 128:256] = (x1 * inv).astype(BF16)
        sd = var * inv
        high = sd.astype(BF16).astype(F32)
        stats = jnp.where(lane(128) == n, high, stats)
        return jnp.where(lane(128) == n + RES, sd - high, stats)

    for copy in weights_in:
        copy.start()
    load[0].wait()
    load[1].wait()
    def send_normed(q):
        def send_a(j, carry):
            row = lax.rem(r + j, ROWS)
            remote(nt.at[q, row], g.at[q, r], s_a.at[q], r_a.at[q], row, c).start()
            return carry

        lax.fori_loop(1, ROWS, send_a, 0)
        pltpu.make_async_copy(nt.at[q, r], g.at[q, r], r_a.at[q]).start()

    def send_sig(j, carry):
        row = lax.rem(r + j, ROWS)
        remote(sig, sg.at[r], s_sig, r_sig, row, c).start()
        return carry

    stats = jnp.zeros((SEQ, 128), F32)
    for q in range(OWN):
        stats = lax.fori_loop(0, ROWS, lambda row, s, q=q: norm_one(q, row, s), stats, unroll=4)
        if q == 0:
            pl.semaphore_wait(barrier, ROWS - 1 + COLS - 1)
            send_normed(0)
            lax.fori_loop(1, COLS, tell, 0)
        if q == 1:
            send_normed(1)
    sig[...] = stats.astype(BF16)
    couplings.start()
    for copy in weights_in:
        copy.wait()

    wit[...] = wi_ref[...].astype(F32).T.astype(BF16)
    wof[...] = wo_ref[...].astype(F32)
    wbd[...] = jnp.zeros(wbd.shape, BF16)

    def spread(d, carry):
        block = wof[pl.ds(d, 32, stride=32), :].astype(BF16)
        for a in range(4):
            at = pl.multiple_of(d * 128 + a * 32, 32)
            wbd[pl.ds(at, 32), a * 128 : (a + 1) * 128] = block
        return carry

    lax.fori_loop(0, 32, spread, 0)
    source = lax.broadcasted_iota(jnp.int32, (512, 512), 0)
    target = ((source >> 5) & 3) * 128 + (source >> 7) * 32 + (source & 31)
    column = lax.broadcasted_iota(jnp.int32, (512, 512), 1)
    perm[...] = jnp.where(column == target, 1.0, 0.0).astype(BF16)

    core = lax.rem(c, 2)

    def slot(q, half):
        return lb.at[q * 16 + core * 8 + lax.rem(c, 8) // 2 * 2 + half]

    def pass_on(q, half):
        def send_l(j, carry):
            col = c // 8 * 8 + lax.rem(c + 2 * j, 8)
            remote(slot(q, half), slot(q, half), s_l, r_l.at[q], r, col).start()
            return carry

        lax.fori_loop(1, 4, send_l, 0)

    def relay(q):
        arrived(lb.at[0], r_h.at[q])
        mine = slot(q, c // 8)
        remote(mine, mine, s_t, r_t.at[q], r, lax.rem(c + 8, COLS)).start()
        pass_on(q, c // 8)

    def relay_twin(q):
        arrived(lb.at[0], r_t.at[q])
        pass_on(q, 1 - c // 8)

    def send_gated(q):
        def send_b(j, carry):
            row = lax.rem(r + j, ROWS)
            remote(gt.at[q, row], gb.at[r * OWN + q], s_b, r_b, row, c).start()
            return carry

        lax.fori_loop(1, ROWS, send_b, 0)
        pltpu.make_async_copy(gt.at[q, r], gb.at[r * OWN + q], r_b).start()

    def share(q):
        arrived(lb.at[pl.ds(0, 6)], r_l.at[q])
        mine = lb.at[pl.ds(q * 16 + core * 8, 8)]
        remote(mine, mine, s_c, r_c.at[q], r, c + 1 - 2 * core).start()

    def attend(q, carry):
        arrived(g.at[q], r_a.at[q])

        @pl.when(q < OWN - 2)
        def _():
            send_normed(q + 2)

        @pl.when(q == 0)
        def _():
            lax.fori_loop(1, ROWS, send_sig, 0)
            pltpu.make_async_copy(sig, sg.at[r], r_sig).start()

        column = g[q].reshape(ALL, FEAT)
        qs[...] = (dot(column, wq_ref[...]) * (32 ** (-0.5) * LOG2E)).astype(BF16)
        kt[...] = dot(column, wx_ref[:, 0:256]).T.astype(BF16)
        vs[...] = dot(column, wx_ref[:, 256:512]).astype(BF16)
        ga[...] = jax.nn.sigmoid(dot(column, wx_ref[:, 512:768]))
        for tile in range(2):
            cols = slice(tile * 128, tile * 128 + 128)
            masks = [head_mask(128, h) for h in range(4)]
            values = jnp.concatenate(
                [
                    jnp.concatenate(
                        [vs[:, cols] * mask, jnp.broadcast_to(mask, (ALL, 128))], axis=1
                    )
                    for mask in masks
                ]
            )
            for part in range(2):
                rows = slice(part * 256, part * 256 + 256)
                weights = []
                for h in range(4):
                    scores = dot(qs[rows, :] * head_mask(256, tile * 4 + h), kt[...])
                    best = jnp.max(scores, axis=-1, keepdims=True)
                    weights.append(jnp.exp2(scores - best).astype(BF16))
                found = dot(jnp.concatenate(weights, axis=1), values)
                gated = (found[:, :128] / found[:, 128:] * ga[rows, cols]).astype(BF16)
                gt[q, part * 4 : part * 4 + 4, :, cols] = gated.reshape(4, SEQ, 128)

        @pl.when(q == 0)
        def _():
            arrived(sg, r_sig)
            pl.semaphore_wait(everyone, COLS - 1)

        for part in range(2):
            rows = slice(part * 256, part * 256 + 256)
            gated = gt[q, part * 4 : part * 4 + 4].reshape(256, FEAT)
            normed = g[q, part * 4 : part * 4 + 4].reshape(256, FEAT).astype(F32)
            spreads = sg[part * 4 : part * 4 + 4].reshape(256, 128).astype(F32)
            n = r * OWN + q
            here = jnp.logical_or(lane(128) == n, lane(128) == n + RES)
            sd = jnp.sum(jnp.where(here, spreads, 0.0), axis=-1, keepdims=True)
            fresh = normed + dot(gated, wf_ref[...]) * (1.0 / sd)
            fresh = fresh - jnp.mean(fresh, axis=-1, keepdims=True)
            var = jnp.mean(fresh * fresh, axis=-1, keepdims=True)
            fresh = (fresh * (sd * lax.rsqrt(sd * sd * var + EPS))).astype(BF16)
            lrs[q, :, rows] = dot_nt(we_ref[...], fresh).astype(BF16)

        spot = q * 16 + lax.rem(r, 2) * 8 + r // 2 * 2 + lax.rem(c, 2)
        meet = lax.rem(c, 2) * 8 + r
        here = jnp.logical_and(rho == r, c == meet)

        @pl.when(here)
        def _():
            pltpu.make_async_copy(lrs.at[q, pl.ds(0, 32)], lb.at[spot], r_h.at[q]).start()

        @pl.when(jnp.logical_not(here))
        def _():
            remote(lrs.at[q, pl.ds(0, 32)], lb.at[spot], s_h, r_h.at[q], rho, meet).start()

        def send_r(j, carry):
            row = lax.rem(r + j, ROWS)
            remote(
                lrs.at[q, pl.ds(32, 32)], rb.at[r * OWN + q], s_r, r_r.at[q], row, c
            ).start()
            return carry

        lax.fori_loop(1, ROWS, send_r, 0)
        pltpu.make_async_copy(lrs.at[q, pl.ds(32, 32)], rb.at[r * OWN + q], r_r.at[q]).start()
        @pl.when(q > 0)
        def _():
            relay(q - 1)

        @pl.when(q > 1)
        def _():
            relay_twin(q - 2)

        @pl.when(q > 2)
        def _():
            share(q - 3)

        return carry

    lax.fori_loop(0, OWN, attend, 0)

    def by_channel(row, q):
        n = row * OWN + q
        for k in range(4):
            rf[k, pl.ds(n, 32, stride=32), :] = rb[n, :, k * 128 : k * 128 + 128].astype(F32)
        return q

    for q in range(OWN):
        if q == OWN - 1:
            relay_twin(OWN - 2)
            relay(OWN - 1)
            share(OWN - 3)
        arrived(rb.at[pl.ds(0, ROWS)], r_r.at[q])
        lax.fori_loop(0, ROWS, by_channel, q, unroll=2)
    for k in range(4):
        rp[:, k * 128 : k * 128 + 128] = rf[k].astype(BF16)

    for q in range(OWN):
        send_gated(q)

    def outer(b, carry):
        left = lb[pl.ds(b * 8, 8)].reshape(256, ALL)
        for d in range(0, 32, 8):
            block = dot_nt(rp[d * 32 : d * 32 + 256, :], left) * (1.0 / ALL)
            block = block.astype(BF16)
            for e in range(8):
                for half in range(2):
                    at = pl.multiple_of(b * 64 + half * 32, 32)
                    om[pl.ds(at, 32), (d + e) * 128 : (d + e + 1) * 128] = block[
                        e * 32 : e * 32 + 32, half * 128 : half * 128 + 128
                    ]
        return carry

    def mid(b):
        update = dot(om[b * 256 : b * 256 + 256, :], wbd[...])
        for f in range(8):
            for a in range(4):
                e, q = f % 4, b * 2 + f // 4
                i = a % 2 * 32 + (e % 2 * 4 + a // 2 * 2 + e // 2) * 4 + q
                pm[q * 16 + e * 4 + a] = (
                    coup[i] + update[f * 32 : f * 32 + 32, a * 128 : a * 128 + 128]
                )

    def entry(b, carry):
        pair = pm[pl.ds(b * 8, 8)].reshape(256, C_Z)
        pair = pair - jnp.mean(pair, axis=-1, keepdims=True)
        var = jnp.mean(pair * pair, axis=-1, keepdims=True)
        pair = (pair * lax.rsqrt(var + EPS)).astype(BF16)
        gp[pl.ds(b * 8, 8)] = jax.nn.sigmoid(dot(pair, wsw_ref[...])).reshape(8, RES, C_Z)
        entries = dot_nt(wit[...], pair)
        left = jax.nn.sigmoid(entries[128:256]) * entries[0:128]
        right = jax.nn.sigmoid(entries[384:512]) * entries[256:384]
        for half in range(2):
            lanes = slice(half * 128, half * 128 + 128)
            t = lax.rem(b, 4) * 2 + half
            cf[b // 4, pl.ds(t, 128, stride=16), :] = left[:, lanes]
            cf[b // 4, pl.ds(t + 8, 128, stride=16), :] = right[:, lanes]
        return carry

    corner = r * 4 + c // 4
    lanes_at = pl.multiple_of(lax.rem(c, 4) * 128, 128)

    def pairs(half):
        for q in (half * 2, half * 2 + 1):
            arrived(lb.at[pl.ds(0, 8)], r_c.at[q])
            lax.fori_loop(q * 2, q * 2 + 2, outer, 0)
            if q == 0:
                relay_twin(OWN - 1)
                share(OWN - 2)
        mid(half)
        lax.fori_loop(half * 4, half * 4 + 4, entry, 0)

    def deal_out(half):
        cb[half] = cf[half].astype(BF16).reshape(DEVICES, 16, 128)

        def send_d(d, carry):
            peer = lax.rem(me + d, DEVICES)
            remote(
                cb.at[half, peer], xlr.at[half, corner, :, pl.ds(lanes_at, 128)],
                s_d.at[half], r_d.at[half], peer // COLS, lax.rem(peer, COLS),
            ).start()
            return carry

        lax.fori_loop(1, DEVICES, send_d, 0)
        pltpu.make_async_copy(
            cb.at[half, me], xlr.at[half, corner, :, pl.ds(lanes_at, 128)], r_d.at[half]
        ).start()

    couplings.wait()
    pairs(0)
    share(OWN - 1)
    deal_out(0)
    pairs(1)
    deal_out(1)

    arrived(gb, r_b)

    def refresh(b, carry):
        change = dot(gb[pl.ds(b * 4, 4)].reshape(256, FEAT), wf_ref[...])
        for e in range(4):
            where = pl.ds(b * 4 + e, SEQ, stride=RES)
            for k in range(2):
                xs[k, where, :] = (
                    xs[k, where, :] + change[e * 64 : e * 64 + 64, k * 128 : k * 128 + 128]
                )
        return carry

    lax.fori_loop(0, RES // 4, refresh, 0)
    store = [
        pltpu.make_async_copy(xs.at[k], out_m.at[:, pl.ds(k * 128, 128)], s_x.at[k])
        for k in range(2)
    ]
    store[0].start()
    store[1].start()

    def line_up(b, half):
        moved = dot(xlr[half, pl.ds(b * 8, 8)].reshape(128, 512), perm[...])
        for e in range(4):
            for a in range(4):
                at = pl.multiple_of(half * 256 + b * 64 + a * 16, 16)
                lanes = slice(a * 128, a * 128 + 128)
                spot = slice(e * 128, e * 128 + 128)
                one, two = moved[e * 16 : e * 16 + 16, lanes], moved[e * 16 + 64 : e * 16 + 80, lanes]
                am[pl.ds(at, 16), spot] = jnp.concatenate([one[:8], two[:8]]).astype(BF16)
                bm[pl.ds(at, 16), spot] = jnp.concatenate([one[8:], two[8:]]).astype(BF16)
        return half

    arrived(xlr.at[0], r_d.at[0])
    lax.fori_loop(0, 4, line_up, 0)
    pa[...] = dot_tn(am[0:256, :], bm[0:256, :])
    arrived(xlr.at[1], r_d.at[1])
    lax.fori_loop(0, 4, line_up, 1)
    pb[...] = (pa[...] + dot_tn(am[256:512, :], bm[256:512, :])).astype(BF16)

    def deal(b, carry):
        row = lax.rem(r + b, ROWS)
        for e in range(4):
            for a in range(4):
                at = pl.multiple_of(row * 64 + a * 16, 16)
                xe[e * 16 : e * 16 + 16, a * 128 : a * 128 + 128] = pb[
                    pl.ds(at, 16), e * 128 : e * 128 + 128
                ]
        es[pl.ds(row * 4, 4)] = dot(xe[...], perm[...]).astype(BF16).reshape(4, 16, 512)

        def piece(col):
            at = pl.multiple_of(lax.rem(col, 4) * 128, 128)
            return es.at[row * 4 + col // 4, :, pl.ds(at, 128)]

        def send_e(j, inner):
            col = lax.rem(c + j, COLS)
            remote(piece(col), er.at[me], s_e, r_e, row, col).start()
            return inner

        lax.fori_loop(1, COLS, send_e, 0)

        @pl.when(b == 0)
        def _():
            pltpu.make_async_copy(piece(c), er.at[me], r_e).start()

        @pl.when(b > 0)
        def _():
            remote(piece(c), er.at[me], s_e, r_e, row, c).start()

        return carry

    lax.fori_loop(0, ROWS, deal, 0)
    arrived(er, r_e)

    ef[...] = er[...].astype(F32).reshape(DEVICES * 16, 128)

    def final(t, carry):
        prod = ef[pl.ds(t, DEVICES, stride=16), :]
        prod = prod - jnp.mean(prod, axis=0, keepdims=True)
        var = jnp.mean(prod * prod, axis=0, keepdims=True)
        prod = (prod * lax.rsqrt(var + EPS)).astype(BF16)
        update = dot_tn(prod, wtri_ref[...])
        for a in range(4):
            p = lax.rem(t, 4) * 16 + lax.rem(t // 4, 2) * 8 + (a % 2 * 2 + t // 8) * 2 + a // 2
            i = a * 16 + t
            coup[i] = pm[p] + gp[p] * update[a * 32 : a * 32 + 32]
            pltpu.make_async_copy(coup.at[i], out_p.at[i], s_o).start()
        return carry

    lax.fori_loop(0, 16, final, 0, unroll=4)

    pltpu.make_async_copy(coup, out_p, s_o).wait()
    store[0].wait()
    store[1].wait()
    for q in range(OWN):
        arrived(nt.at[q, pl.ds(0, 7)], s_a.at[q])
    arrived(sg.at[pl.ds(0, 7)], s_sig)
    arrived(gb.at[pl.ds(0, 28)], s_b)
    arrived(rb.at[pl.ds(0, 28)], s_r)


    @pl.when(jnp.logical_not(jnp.logical_and(rho == r, lax.rem(c, 2) * 8 + r == c)))
    def _():
        arrived(lb.at[pl.ds(0, OWN)], s_h)

    arrived(lb.at[pl.ds(0, OWN)], s_t)
    arrived(lb.at[pl.ds(0, 24)], s_l)
    arrived(lb.at[pl.ds(0, 32)], s_c)
    for half in range(2):
        arrived(cb.at[half, pl.ds(0, DEVICES - 1)], s_d.at[half])
    arrived(er.at[pl.ds(0, DEVICES - 1)], s_e)


def hand_over(m_ref, p_ref, out_m, out_p, m, p, sems):
    def pieces(source, held, result, count, first):
        rows = held.shape[0] // count
        for k in range(count):
            at = pl.ds(k * rows, rows)
            yield (
                pltpu.make_async_copy(source.at[at], held.at[at], sems.at[first + k]),
                pltpu.make_async_copy(held.at[at], result.at[at], sems.at[first + k]),
            )

    copies = list(pieces(m_ref, m, out_m, 8, 0)) + list(pieces(p_ref, p, out_p, 4, 8))
    for load, _ in copies:
        load.start()
    for load, store in copies:
        load.wait()
        store.start()
    for _, store in copies:
        store.wait()


def body(x, coup, wq, wx, wf, we, wo, wi, wsw, wtri):
    weights = (wq, wx, wf, we.T, wo, wi, wsw, wtri)
    hbm = pl.BlockSpec(memory_space=pl.ANY)
    dma = pltpu.SemaphoreType.DMA
    out_m, out_p = pl.pallas_call(
        kernel,
        out_shape=(
            jax.ShapeDtypeStruct((SEQ * RES, FEAT), F32),
            jax.ShapeDtypeStruct((SEQ, RES, C_Z), F32),
        ),
        in_specs=[hbm] * 10,
        out_specs=(hbm, hbm),
        scratch_shapes=[pltpu.VMEM(w.shape, BF16) for w in weights]
        + [
            pltpu.VMEM((2, SEQ * RES, 128), F32),
            pltpu.VMEM((SEQ, RES, C_Z), F32),
            pltpu.VMEM((OWN, ROWS, SEQ, FEAT), BF16),
            pltpu.VMEM((OWN, ROWS, SEQ, FEAT), BF16),
            pltpu.VMEM((SEQ, 128), BF16),
            pltpu.VMEM((ROWS, SEQ, 128), BF16),
            pltpu.VMEM((ALL, FEAT), BF16),
            pltpu.VMEM((FEAT, ALL), BF16),
            pltpu.VMEM((ALL, FEAT), BF16),
            pltpu.VMEM((ALL, FEAT), F32),
            pltpu.VMEM((OWN, ROWS, SEQ, FEAT), BF16),
            pltpu.VMEM((RES, SEQ, FEAT), BF16),
            pltpu.VMEM((OWN, 64, ALL), BF16),
            pltpu.VMEM((RES, 32, ALL), BF16),
            pltpu.VMEM((SEQ, 32, ALL), BF16),
            pltpu.VMEM((512, C_Z), BF16),
            pltpu.VMEM((1024, C_Z), F32),
            pltpu.VMEM((4096, 512), BF16),
            pltpu.VMEM((512, 512), BF16),
            pltpu.VMEM((4, 1024, 128), F32),
            pltpu.VMEM((1024, ALL), BF16),
            pltpu.VMEM((512, 4096), BF16),
            pltpu.VMEM((SEQ, RES, C_Z), F32),
            pltpu.VMEM((SEQ, RES, C_Z), F32),
            pltpu.VMEM((2, DEVICES * 16, 128), F32),
            pltpu.VMEM((2, DEVICES, 16, 128), BF16),
            pltpu.VMEM((2, 32, 16, 512), BF16),
            pltpu.VMEM((512, 512), BF16),
            pltpu.VMEM((512, 512), BF16),
            pltpu.VMEM((512, 512), F32),
            pltpu.VMEM((512, 512), BF16),
            pltpu.VMEM((64, 512), BF16),
            pltpu.VMEM((32, 16, 512), BF16),
            pltpu.VMEM((DEVICES, 16, 128), BF16),
            pltpu.VMEM((DEVICES * 16, 128), F32),
            pltpu.SemaphoreType.REGULAR,
            dma((2,)),
            dma(()),
            dma((8,)),
            dma(()),
            dma((OWN,)), dma((OWN,)),
            dma(()), dma(()),
            dma(()), dma(()),
            dma(()), dma((OWN,)),
            dma(()), dma((OWN,)),
            dma(()), dma((OWN,)),
            dma(()), dma((OWN,)),
            dma(()), dma((OWN,)),
            dma((2,)), dma((2,)),
            dma(()), dma(()),
        ],
        compiler_params=pltpu.CompilerParams(
            collective_id=0, has_side_effects=True, vmem_limit_bytes=56 * 2**20
        ),
    )(x.reshape(SEQ * RES, FEAT), coup, *weights)
    out_m, out_p = pl.pallas_call(
        hand_over,
        out_shape=(
            jax.ShapeDtypeStruct((SEQ * RES, FEAT), F32),
            jax.ShapeDtypeStruct((SEQ, RES, C_Z), F32),
        ),
        in_specs=[hbm] * 2,
        out_specs=(hbm, hbm),
        scratch_shapes=[
            pltpu.VMEM((SEQ * RES, FEAT), F32), pltpu.VMEM((SEQ, RES, C_Z), F32), dma((12,)),
        ],
    )(out_m, out_p)
    return out_m.reshape(SEQ, RES, FEAT), out_p


def solution(mesh):
    spread = P("row", "col", None)
    return jax.shard_map(
        body, mesh=mesh, in_specs=(spread, spread) + (P(),) * 8,
        out_specs=(spread, spread), check_vma=False,
    )
```

```python
import functools

import jax
import jax.numpy as jnp
from jax import lax
from jax.experimental import pallas as pl
from jax.experimental.pallas import tpu as pltpu
from jax.sharding import PartitionSpec as P

F32, BF16 = jnp.float32, jnp.bfloat16
MESH = pl.DeviceIdType.MESH
EPS = 1e-05
LOG2E = 1.4426950408889634
ROWS, COLS = 8, 16
DEVICES = ROWS * COLS
SEQ, RES = 64, 32
OWN = 4
ALL = 512
FEAT, HEADS = 256, 8
C_Z = 128


def dot(a, b):
    return jnp.dot(a, b, preferred_element_type=F32)


def dot_nt(a, b):
    return lax.dot_general(a, b, (((1,), (1,)), ((), ())), preferred_element_type=F32)


def dot_tn(a, b):
    return lax.dot_general(a, b, (((0,), (0,)), ((), ())), preferred_element_type=F32)


def lane(width):
    return lax.broadcasted_iota(jnp.int32, (1, width), 1)


def head_mask(width, which):
    return jnp.where((lane(width) >> 5) == which, 1.0, 0.0).astype(BF16)


def kernel(
    x_ref, coup_ref, wq_in, wx_in, wf_in, we_in, wo_in, wi_in, wsw_in, wtri_in,
    out_m, out_p,
    wq_ref, wx_ref, wf_ref, we_ref, wo_ref, wi_ref, wsw_ref, wtri_ref,
    xs, coup, nt, g, sig, sg, qs, kt, vs, ga, gt, gb, lrs, rb, lb,
    wit, wof, wbd, perm, rf, rp, om, pm, gp, cf, cb, xlr, am, bm, pa, pb, xe, es, er, ef,
    everyone, s_x, s_c0, s_w, s_o, s_a, r_a, s_sig, r_sig, s_b, r_b, s_h, r_h, s_t, r_t, s_l, r_l, s_c, r_c, s_r, r_r, s_d, r_d, s_e, r_e,
):
    r = lax.axis_index("row")
    c = lax.axis_index("col")
    me = r * COLS + c
    rho = c // 2

    def remote(src, dst, send, recv, row, col):
        return pltpu.make_async_remote_copy(
            src_ref=src, dst_ref=dst, send_sem=send, recv_sem=recv,
            device_id=(row, col), device_id_type=MESH,
        )

    def arrived(ref, sem):
        pltpu.make_async_copy(ref, ref, sem).wait()

    load = [
        pltpu.make_async_copy(x_ref.at[:, pl.ds(k * 128, 128)], xs.at[k, pl.ds(0, SEQ * RES)], s_x.at[k])
        for k in range(2)
    ]
    load[0].start()
    load[1].start()
    couplings = pltpu.make_async_copy(coup_ref, coup, s_c0)
    weights_in = [
        pltpu.make_async_copy(source, held, s_w.at[k])
        for k, (source, held) in enumerate(
            (
                (wq_in, wq_ref), (wx_in, wx_ref), (wf_in, wf_ref), (we_in, we_ref),
                (wo_in, wo_ref), (wi_in, wi_ref), (wsw_in, wsw_ref), (wtri_in, wtri_ref),
            )
        )
    ]

    barrier = pltpu.get_barrier_semaphore()

    def greet_along_row(d, carry):
        pl.semaphore_signal(
            barrier, inc=1, device_id=(lax.rem(r + d, ROWS), c), device_id_type=MESH
        )
        return carry

    def greet_along_col(d, carry):
        pl.semaphore_signal(
            barrier, inc=1, device_id=(r, lax.rem(c + d, COLS)), device_id_type=MESH
        )
        return carry

    lax.fori_loop(1, ROWS, greet_along_row, 0)
    lax.fori_loop(1, COLS, greet_along_col, 0)

    def tell(d, carry):
        pl.semaphore_signal(
            everyone, inc=1, device_id=(r, lax.rem(c + d, COLS)), device_id_type=MESH
        )
        return carry

    def norm_one(q, row, stats):
        n = row * OWN + q
        x0 = xs[0, pl.ds(n, SEQ, stride=RES), :]
        x1 = xs[1, pl.ds(n, SEQ, stride=RES), :]
        mean = jnp.sum(x0 + x1, axis=-1, keepdims=True) * (1.0 / FEAT)
        x0, x1 = x0 - mean, x1 - mean
        var = jnp.sum(x0 * x0 + x1 * x1, axis=-1, keepdims=True) * (1.0 / FEAT) + EPS
        inv = lax.rsqrt(var)
        nt[q, row, :, 0:128] = (x0 * inv).astype(BF16)
        nt[q, row, :, 128:256] = (x1 * inv).astype(BF16)
        sd = var * inv
        high = sd.astype(BF16).astype(F32)
        stats = jnp.where(lane(128) == n, high, stats)
        return jnp.where(lane(128) == n + RES, sd - high, stats)

    for copy in weights_in:
        copy.start()
    load[0].wait()
    load[1].wait()
    def send_normed(q):
        def send_a(j, carry):
            row = lax.rem(r + j, ROWS)
            remote(nt.at[q, row], g.at[q, r], s_a.at[q], r_a.at[q], row, c).start()
            return carry

        lax.fori_loop(1, ROWS, send_a, 0)
        pltpu.make_async_copy(nt.at[q, r], g.at[q, r], r_a.at[q]).start()

    def send_sig(j, carry):
        row = lax.rem(r + j, ROWS)
        remote(sig, sg.at[r], s_sig, r_sig, row, c).start()
        return carry

    stats = jnp.zeros((SEQ, 128), F32)
    for q in range(OWN):
        stats = lax.fori_loop(0, ROWS, lambda row, s, q=q: norm_one(q, row, s), stats, unroll=4)
        if q == 0:
            pl.semaphore_wait(barrier, ROWS - 1 + COLS - 1)
            send_normed(0)
            lax.fori_loop(1, COLS, tell, 0)
        if q == 1:
            send_normed(1)
    sig[...] = stats.astype(BF16)
    couplings.start()
    for copy in weights_in:
        copy.wait()

    wit[...] = wi_ref[...].astype(F32).T.astype(BF16)
    wof[0:1024] = wo_ref[...].astype(F32)
    wbd[...] = jnp.zeros(wbd.shape, BF16)

    def spread(d, carry):
        block = wof[pl.ds(d, 32, stride=32), :].astype(BF16)
        for a in range(4):
            at = pl.multiple_of(d * 128 + a * 32, 32)
            wbd[pl.ds(at, 32), a * 128 : (a + 1) * 128] = block
        return carry

    lax.fori_loop(0, 32, spread, 0)
    source = lax.broadcasted_iota(jnp.int32, (512, 512), 0)
    target = ((source >> 5) & 3) * 128 + (source >> 7) * 32 + (source & 31)
    column = lax.broadcasted_iota(jnp.int32, (512, 512), 1)
    perm[...] = jnp.where(column == target, 1.0, 0.0).astype(BF16)

    core = lax.rem(c, 2)

    def slot(q, half):
        return lb.at[q * 16 + core * 8 + lax.rem(c, 8) // 2 * 2 + half]

    def pass_on(q, half):
        def send_l(j, carry):
            col = c // 8 * 8 + lax.rem(c + 2 * j, 8)
            remote(slot(q, half), slot(q, half), s_l, r_l.at[q], r, col).start()
            return carry

        lax.fori_loop(1, 4, send_l, 0)

    def relay(q):
        arrived(lb.at[0], r_h.at[q])
        mine = slot(q, c // 8)
        remote(mine, mine, s_t, r_t.at[q], r, lax.rem(c + 8, COLS)).start()
        pass_on(q, c // 8)

    def relay_twin(q):
        arrived(lb.at[0], r_t.at[q])
        pass_on(q, 1 - c // 8)

    def send_gated(q):
        def send_b(j, carry):
            row = lax.rem(r + j, ROWS)
            remote(gt.at[q, row], gb.at[r * OWN + q], s_b, r_b, row, c).start()
            return carry

        lax.fori_loop(1, ROWS, send_b, 0)
        pltpu.make_async_copy(gt.at[q, r], gb.at[r * OWN + q], r_b).start()

    def share(q):
        arrived(lb.at[pl.ds(0, 6)], r_l.at[q])
        mine = lb.at[pl.ds(q * 16 + core * 8, 8)]
        remote(mine, mine, s_c, r_c.at[q], r, c + 1 - 2 * core).start()

    def attend(q, carry):
        arrived(g.at[q], r_a.at[q])

        @pl.when(q < OWN - 2)
        def _():
            send_normed(q + 2)

        @pl.when(q == 0)
        def _():
            lax.fori_loop(1, ROWS, send_sig, 0)
            pltpu.make_async_copy(sig, sg.at[r], r_sig).start()

        column = g[q].reshape(ALL, FEAT)
        qs[...] = (dot(column, wq_ref[...]) * (32 ** (-0.5) * LOG2E)).astype(BF16)
        kt[...] = dot(column, wx_ref[:, 0:256]).T.astype(BF16)
        vs[...] = dot(column, wx_ref[:, 256:512]).astype(BF16)
        ga[...] = jax.nn.sigmoid(dot(column, wx_ref[:, 512:768]))
        for tile in range(2):
            cols = slice(tile * 128, tile * 128 + 128)
            masks = [head_mask(128, h) for h in range(4)]
            values = jnp.concatenate(
                [
                    jnp.concatenate(
                        [vs[:, cols] * mask, jnp.broadcast_to(mask, (ALL, 128))], axis=1
                    )
                    for mask in masks
                ]
            )
            for part in range(2):
                rows = slice(part * 256, part * 256 + 256)
                weights = []
                for h in range(4):
                    scores = dot(qs[rows, :] * head_mask(256, tile * 4 + h), kt[...])
                    best = jnp.max(scores, axis=-1, keepdims=True)
                    weights.append(jnp.exp2(scores - best).astype(BF16))
                found = dot(jnp.concatenate(weights, axis=1), values)
                gated = (found[:, :128] / found[:, 128:] * ga[rows, cols]).astype(BF16)
                gt[q, part * 4 : part * 4 + 4, :, cols] = gated.reshape(4, SEQ, 128)

        @pl.when(q == 0)
        def _():
            arrived(sg, r_sig)
            pl.semaphore_wait(everyone, COLS - 1)

        for part in range(2):
            rows = slice(part * 256, part * 256 + 256)
            gated = gt[q, part * 4 : part * 4 + 4].reshape(256, FEAT)
            normed = g[q, part * 4 : part * 4 + 4].reshape(256, FEAT).astype(F32)
            spreads = sg[part * 4 : part * 4 + 4].reshape(256, 128).astype(F32)
            n = r * OWN + q
            here = jnp.logical_or(lane(128) == n, lane(128) == n + RES)
            sd = jnp.sum(jnp.where(here, spreads, 0.0), axis=-1, keepdims=True)
            fresh = normed + dot(gated, wf_ref[...]) * (1.0 / sd)
            fresh = fresh - jnp.mean(fresh, axis=-1, keepdims=True)
            var = jnp.mean(fresh * fresh, axis=-1, keepdims=True)
            fresh = (fresh * (sd * lax.rsqrt(sd * sd * var + EPS))).astype(BF16)
            lrs[q, :, rows] = dot_nt(we_ref[...], fresh).astype(BF16)

        spot = q * 16 + lax.rem(r, 2) * 8 + r // 2 * 2 + lax.rem(c, 2)
        meet = lax.rem(c, 2) * 8 + r
        here = jnp.logical_and(rho == r, c == meet)

        @pl.when(here)
        def _():
            pltpu.make_async_copy(lrs.at[q, pl.ds(0, 32)], lb.at[spot], r_h.at[q]).start()

        @pl.when(jnp.logical_not(here))
        def _():
            remote(lrs.at[q, pl.ds(0, 32)], lb.at[spot], s_h, r_h.at[q], rho, meet).start()

        def send_r(j, carry):
            row = lax.rem(r + j, ROWS)
            remote(
                lrs.at[q, pl.ds(32, 32)], rb.at[r * OWN + q], s_r, r_r.at[q], row, c
            ).start()
            return carry

        lax.fori_loop(1, ROWS, send_r, 0)
        pltpu.make_async_copy(lrs.at[q, pl.ds(32, 32)], rb.at[r * OWN + q], r_r.at[q]).start()
        @pl.when(q > 0)
        def _():
            relay(q - 1)

        @pl.when(q > 1)
        def _():
            relay_twin(q - 2)

        @pl.when(q > 2)
        def _():
            share(q - 3)

        return carry

    lax.fori_loop(0, OWN, attend, 0)

    def by_channel(row, q):
        n = row * OWN + q
        for k in range(4):
            rf[k, pl.ds(n, 32, stride=32), :] = rb[n, :, k * 128 : k * 128 + 128].astype(F32)
        return q

    for q in range(OWN):
        if q == OWN - 1:
            relay_twin(OWN - 2)
            relay(OWN - 1)
            share(OWN - 3)
        arrived(rb.at[pl.ds(0, ROWS)], r_r.at[q])
        lax.fori_loop(0, ROWS, by_channel, q, unroll=2)
    for k in range(4):
        rp[:, k * 128 : k * 128 + 128] = rf[k, 0:1024].astype(BF16)

    for q in range(OWN):
        send_gated(q)

    def outer(b, carry):
        left = lb[pl.ds(b * 8, 8)].reshape(256, ALL)
        for d in range(0, 32, 8):
            block = dot_nt(rp[d * 32 : d * 32 + 256, :], left) * (1.0 / ALL)
            block = block.astype(BF16)
            for e in range(8):
                for half in range(2):
                    at = pl.multiple_of(b * 64 + half * 32, 32)
                    om[pl.ds(at, 32), (d + e) * 128 : (d + e + 1) * 128] = block[
                        e * 32 : e * 32 + 32, half * 128 : half * 128 + 128
                    ]
        return carry

    def mid(b):
        update = dot(om[b * 256 : b * 256 + 256, :], wbd[...])
        for f in range(8):
            for a in range(4):
                e, q = f % 4, b * 2 + f // 4
                i = a % 2 * 32 + (e % 2 * 4 + a // 2 * 2 + e // 2) * 4 + q
                pm[q * 16 + e * 4 + a] = (
                    coup[i] + update[f * 32 : f * 32 + 32, a * 128 : a * 128 + 128]
                )

    def entry(b, carry):
        pair = pm[pl.ds(b * 8, 8)].reshape(256, C_Z)
        pair = pair - jnp.mean(pair, axis=-1, keepdims=True)
        var = jnp.mean(pair * pair, axis=-1, keepdims=True)
        pair = (pair * lax.rsqrt(var + EPS)).astype(BF16)
        gp[pl.ds(b * 8, 8)] = jax.nn.sigmoid(dot(pair, wsw_ref[...])).reshape(8, RES, C_Z)
        entries = dot_nt(wit[...], pair)
        left = jax.nn.sigmoid(entries[128:256]) * entries[0:128]
        right = jax.nn.sigmoid(entries[384:512]) * entries[256:384]
        for half in range(2):
            lanes = slice(half * 128, half * 128 + 128)
            t = lax.rem(b, 4) * 2 + half
            cf[b // 4, pl.ds(t, 128, stride=16), :] = left[:, lanes]
            cf[b // 4, pl.ds(t + 8, 128, stride=16), :] = right[:, lanes]
        return carry

    corner = r * 4 + c // 4
    lanes_at = pl.multiple_of(lax.rem(c, 4) * 128, 128)

    def pairs(half):
        for q in (half * 2, half * 2 + 1):
            arrived(lb.at[pl.ds(0, 8)], r_c.at[q])
            lax.fori_loop(q * 2, q * 2 + 2, outer, 0)
            if q == 0:
                relay_twin(OWN - 1)
                share(OWN - 2)
        mid(half)
        lax.fori_loop(half * 4, half * 4 + 4, entry, 0)

    def deal_out(half):
        cb[half] = cf[half, 0 : DEVICES * 16].astype(BF16).reshape(DEVICES, 16, 128)

        def send_d(d, carry):
            peer = lax.rem(me + d, DEVICES)
            remote(
                cb.at[half, peer], xlr.at[half, corner, :, pl.ds(lanes_at, 128)],
                s_d.at[half], r_d.at[half], peer // COLS, lax.rem(peer, COLS),
            ).start()
            return carry

        lax.fori_loop(1, DEVICES, send_d, 0)
        pltpu.make_async_copy(
            cb.at[half, me], xlr.at[half, corner, :, pl.ds(lanes_at, 128)], r_d.at[half]
        ).start()

    couplings.wait()
    pairs(0)
    share(OWN - 1)
    deal_out(0)
    pairs(1)
    deal_out(1)

    arrived(gb, r_b)

    def refresh(b, carry):
        change = dot(gb[pl.ds(b * 4, 4)].reshape(256, FEAT), wf_ref[...])
        for e in range(4):
            where = pl.ds(b * 4 + e, SEQ, stride=RES)
            for k in range(2):
                xs[k, where, :] = (
                    xs[k, where, :] + change[e * 64 : e * 64 + 64, k * 128 : k * 128 + 128]
                )
        return carry

    lax.fori_loop(0, RES // 4, refresh, 0)
    store = [
        pltpu.make_async_copy(xs.at[k, pl.ds(0, SEQ * RES)], out_m.at[:, pl.ds(k * 128, 128)], s_x.at[k])
        for k in range(2)
    ]
    store[0].start()
    store[1].start()

    def line_up(b, half):
        moved = dot(xlr[half, pl.ds(b * 8, 8)].reshape(128, 512), perm[...])
        for e in range(4):
            for a in range(4):
                at = pl.multiple_of(half * 256 + b * 64 + a * 16, 16)
                lanes = slice(a * 128, a * 128 + 128)
                spot = slice(e * 128, e * 128 + 128)
                one, two = moved[e * 16 : e * 16 + 16, lanes], moved[e * 16 + 64 : e * 16 + 80, lanes]
                am[pl.ds(at, 16), spot] = jnp.concatenate([one[:8], two[:8]]).astype(BF16)
                bm[pl.ds(at, 16), spot] = jnp.concatenate([one[8:], two[8:]]).astype(BF16)
        return half

    arrived(xlr.at[0], r_d.at[0])
    lax.fori_loop(0, 4, line_up, 0)
    pa[...] = dot_tn(am[0:256, :], bm[0:256, :])
    arrived(xlr.at[1], r_d.at[1])
    lax.fori_loop(0, 4, line_up, 1)
    pb[...] = (pa[...] + dot_tn(am[256:512, :], bm[256:512, :])).astype(BF16)

    def deal(b, carry):
        row = lax.rem(r + b, ROWS)
        for e in range(4):
            for a in range(4):
                at = pl.multiple_of(row * 64 + a * 16, 16)
                xe[e * 16 : e * 16 + 16, a * 128 : a * 128 + 128] = pb[
                    pl.ds(at, 16), e * 128 : e * 128 + 128
                ]
        es[pl.ds(row * 4, 4)] = dot(xe[...], perm[...]).astype(BF16).reshape(4, 16, 512)

        def piece(col):
            at = pl.multiple_of(lax.rem(col, 4) * 128, 128)
            return es.at[row * 4 + col // 4, :, pl.ds(at, 128)]

        def send_e(j, inner):
            col = lax.rem(c + j, COLS)
            remote(piece(col), er.at[me], s_e, r_e, row, col).start()
            return inner

        lax.fori_loop(1, COLS, send_e, 0)

        @pl.when(b == 0)
        def _():
            pltpu.make_async_copy(piece(c), er.at[me], r_e).start()

        @pl.when(b > 0)
        def _():
            remote(piece(c), er.at[me], s_e, r_e, row, c).start()

        return carry

    lax.fori_loop(0, ROWS, deal, 0)
    arrived(er, r_e)

    ef[0 : DEVICES * 16] = er[...].astype(F32).reshape(DEVICES * 16, 128)

    def final(t, carry):
        prod = ef[pl.ds(t, DEVICES, stride=16), :]
        prod = prod - jnp.mean(prod, axis=0, keepdims=True)
        var = jnp.mean(prod * prod, axis=0, keepdims=True)
        prod = (prod * lax.rsqrt(var + EPS)).astype(BF16)
        update = dot_tn(prod, wtri_ref[...])
        for a in range(4):
            p = lax.rem(t, 4) * 16 + lax.rem(t // 4, 2) * 8 + (a % 2 * 2 + t // 8) * 2 + a // 2
            i = a * 16 + t
            coup[i] = pm[p] + gp[p] * update[a * 32 : a * 32 + 32]
            pltpu.make_async_copy(coup.at[i], out_p.at[i], s_o).start()
        return carry

    lax.fori_loop(0, 16, final, 0, unroll=4)

    pltpu.make_async_copy(coup, out_p, s_o).wait()
    store[0].wait()
    store[1].wait()
    for q in range(OWN):
        arrived(nt.at[q, pl.ds(0, 7)], s_a.at[q])
    arrived(sg.at[pl.ds(0, 7)], s_sig)
    arrived(gb.at[pl.ds(0, 28)], s_b)
    arrived(rb.at[pl.ds(0, 28)], s_r)


    @pl.when(jnp.logical_not(jnp.logical_and(rho == r, lax.rem(c, 2) * 8 + r == c)))
    def _():
        arrived(lb.at[pl.ds(0, OWN)], s_h)

    arrived(lb.at[pl.ds(0, OWN)], s_t)
    arrived(lb.at[pl.ds(0, 24)], s_l)
    arrived(lb.at[pl.ds(0, 32)], s_c)
    for half in range(2):
        arrived(cb.at[half, pl.ds(0, DEVICES - 1)], s_d.at[half])
    arrived(er.at[pl.ds(0, DEVICES - 1)], s_e)


def hand_over(m_ref, p_ref, out_m, out_p, m, p, sems):
    def pieces(source, held, result, count, first):
        rows = held.shape[0] // count
        for k in range(count):
            at = pl.ds(k * rows, rows)
            yield (
                pltpu.make_async_copy(source.at[at], held.at[at], sems.at[first + k]),
                pltpu.make_async_copy(held.at[at], result.at[at], sems.at[first + k]),
            )

    copies = list(pieces(m_ref, m, out_m, 8, 0)) + list(pieces(p_ref, p, out_p, 4, 8))
    for load, _ in copies:
        load.start()
    for load, store in copies:
        load.wait()
        store.start()
    for _, store in copies:
        store.wait()


def body(x, coup, wq, wx, wf, we, wo, wi, wsw, wtri):
    weights = (wq, wx, wf, we.T, wo, wi, wsw, wtri)
    hbm = pl.BlockSpec(memory_space=pl.ANY)
    dma = pltpu.SemaphoreType.DMA
    out_m, out_p = pl.pallas_call(
        kernel,
        out_shape=(
            jax.ShapeDtypeStruct((SEQ * RES, FEAT), F32),
            jax.ShapeDtypeStruct((SEQ, RES, C_Z), F32),
        ),
        in_specs=[hbm] * 10,
        out_specs=(hbm, hbm),
        scratch_shapes=[pltpu.VMEM(w.shape, BF16) for w in weights]
        + [
            pltpu.VMEM((2, SEQ * RES + RES, 128), F32),
            pltpu.VMEM((SEQ, RES, C_Z), F32),
            pltpu.VMEM((OWN, ROWS, SEQ, FEAT), BF16),
            pltpu.VMEM((OWN, ROWS, SEQ, FEAT), BF16),
            pltpu.VMEM((SEQ, 128), BF16),
            pltpu.VMEM((ROWS, SEQ, 128), BF16),
            pltpu.VMEM((ALL, FEAT), BF16),
            pltpu.VMEM((FEAT, ALL), BF16),
            pltpu.VMEM((ALL, FEAT), BF16),
            pltpu.VMEM((ALL, FEAT), F32),
            pltpu.VMEM((OWN, ROWS, SEQ, FEAT), BF16),
            pltpu.VMEM((RES, SEQ, FEAT), BF16),
            pltpu.VMEM((OWN, 64, ALL), BF16),
            pltpu.VMEM((RES, 32, ALL), BF16),
            pltpu.VMEM((SEQ, 32, ALL), BF16),
            pltpu.VMEM((512, C_Z), BF16),
            pltpu.VMEM((1024 + 32, C_Z), F32),
            pltpu.VMEM((4096, 512), BF16),
            pltpu.VMEM((512, 512), BF16),
            pltpu.VMEM((4, 1024 + 32, 128), F32),
            pltpu.VMEM((1024, ALL), BF16),
            pltpu.VMEM((512, 4096), BF16),
            pltpu.VMEM((SEQ, RES, C_Z), F32),
            pltpu.VMEM((SEQ, RES, C_Z), F32),
            pltpu.VMEM((2, DEVICES * 16 + 16, 128), F32),
            pltpu.VMEM((2, DEVICES, 16, 128), BF16),
            pltpu.VMEM((2, 32, 16, 512), BF16),
            pltpu.VMEM((512, 512), BF16),
            pltpu.VMEM((512, 512), BF16),
            pltpu.VMEM((512, 512), F32),
            pltpu.VMEM((512, 512), BF16),
            pltpu.VMEM((64, 512), BF16),
            pltpu.VMEM((32, 16, 512), BF16),
            pltpu.VMEM((DEVICES, 16, 128), BF16),
            pltpu.VMEM((DEVICES * 16 + 16, 128), F32),
            pltpu.SemaphoreType.REGULAR,
            dma((2,)),
            dma(()),
            dma((8,)),
            dma(()),
            dma((OWN,)), dma((OWN,)),
            dma(()), dma(()),
            dma(()), dma(()),
            dma(()), dma((OWN,)),
            dma(()), dma((OWN,)),
            dma(()), dma((OWN,)),
            dma(()), dma((OWN,)),
            dma(()), dma((OWN,)),
            dma((2,)), dma((2,)),
            dma(()), dma(()),
        ],
        compiler_params=pltpu.CompilerParams(
            collective_id=0, has_side_effects=True, vmem_limit_bytes=56 * 2**20
        ),
    )(x.reshape(SEQ * RES, FEAT), coup, *weights)
    out_m, out_p = pl.pallas_call(
        hand_over,
        out_shape=(
            jax.ShapeDtypeStruct((SEQ * RES, FEAT), F32),
            jax.ShapeDtypeStruct((SEQ, RES, C_Z), F32),
        ),
        in_specs=[hbm] * 2,
        out_specs=(hbm, hbm),
        scratch_shapes=[
            pltpu.VMEM((SEQ * RES, FEAT), F32), pltpu.VMEM((SEQ, RES, C_Z), F32), dma((12,)),
        ],
    )(out_m, out_p)
    return out_m.reshape(SEQ, RES, FEAT), out_p


def solution(mesh):
    spread = P("row", "col", None)
    return jax.shard_map(
        body, mesh=mesh, in_specs=(spread, spread) + (P(),) * 8,
        out_specs=(spread, spread), check_vma=False,
    )
```
